256 devices in a mesh: north: 32 (over y, z), east: 8 (over x, core).
Axes of the slice: x: 4, y: 4, z: 8, core: 2. Of those that a mesh axis runs over, the one named last changes fastest.
Arguments:
- head_ensemble: float32 [2, 64, 1024, 1024], P(None, None, 'north', 'east'), may hold values from -6 to 6
- transmissivity_grid: float32 [2, 1024, 1024], P(None, 'north', 'east'), may hold values from 0.02 to 0.08
- interlayer_leakage_factor: float32 [1024, 1024], P('north', 'east'), may hold values from 0.05 to 0.3
- specific_porosity_release: float32 [1024, 1024], P('north', 'east'), may hold values from 0.3 to 1.5
- infiltration_inflow: float32 [1024, 1024], P('north', 'east'), may hold values from -1.8 to 1.8
- obs_value: float32 [2, 4, 32, 32], replicated, may hold values from -6 to 6
- obs_error: float32 [2, 4, 32, 32], replicated, may hold values from 0.1 to 1
- obs_spot: int32 [2, 4, 32, 32], replicated, may hold values from 0 to 255
- obs_live: int32 [2, 4, 32, 32], replicated, may hold values from 0 to 1
- batch_colour: int32 [2, 4], replicated, may hold values from 0 to 3, as said below
Outputs:
- analysed: float32 [2, 64, 1024, 1024], P(None, None, 'north', 'east')
The draws below stay inside these ranges and needn't reach their ends.
Inputs may be any that keep to these rules, and one draw needn't show every extreme that they name: `obs_spot`: position of the observation in its coarse cell, as row * 16 + column. `batch_colour`: each row is an order of the four colours.
All inputs are finite; a program needn't handle non-finite values.
Results may differ from the reference program's by a relative error of at most 0.0001.
Values sent between devices are 32-bit elements; how exact they have to be, the bound alone decides.
No kernel may reach another device: no remote copies, remote signals or barrier semaphores. Data moves between devices by JAX's collectives and lax.ppermute only.
A program may use at most 128 MiB of HBM per device.

```python
import math
import jax
import jax.numpy as jnp
from jax import lax

MEMBERS = 64
AQUIFER_LAYERS = 2
ITERS = 3
ANALYSES = 2
BATCHES = 4
RADIUS = 8
SPAN = 16
ROWS = 1024
COLS = 1024
LAT_ROWS = 32
LAT_COLS = 32


def draw_obs_live(key, part):
    key = jax.random.fold_in(key, 11)
    scores = jax.random.randint(key, (ANALYSES, BATCHES, LAT_ROWS, LAT_COLS), 0, 100)
    lattice = jnp.arange(LAT_ROWS, dtype=jnp.int32)
    threshold = 90 - 75 * lattice // max(LAT_ROWS - 1, 1)
    return (scores < threshold[None, None, :, None]).astype(jnp.int32)


def draw_batch_colour(key, part):
    key = jax.random.fold_in(key, 23)
    orders = [jax.random.permutation(jax.random.fold_in(key, cycle), BATCHES) for cycle in range(ANALYSES)]
    return jnp.stack(orders).astype(jnp.int32)


def set_ends(drawn, stream_key, low, largest):
    index_at = [jax.random.randint(jax.random.fold_in(stream_key, axis), (), 0, length) for axis, length in enumerate(drawn.shape)]
    widest = drawn.shape.index(max(drawn.shape))
    neighbour = index_at[:widest] + [(index_at[widest] + 1) % drawn.shape[widest]] + index_at[widest + 1:]
    return drawn.at[tuple(index_at)].set(low).at[tuple(neighbour)].set(largest)


def levels(stream_key, dims, split, least, largest):
    factor_of = 1.0
    for position, parts in split:
        steps = jax.random.uniform(jax.random.fold_in(jax.random.fold_in(stream_key, 6), position), (parts,), jnp.float32, least / len(split), largest / len(split))
        factor_of = factor_of * jnp.repeat(jnp.exp(steps), dims[position] // parts).reshape((-1,) + (1,) * (len(dims) - 1 - position))
    return factor_of


def scatter_about(key, dims, scale, bound, shards=(), kind=jnp.bfloat16):
    entries = jax.random.normal(key, dims, jnp.float32) * scale
    if len(shards) > 0:
        entries = levels(key, dims, shards, -0.22, 0.18) * entries
    return jnp.clip(entries, min=-bound, max=bound).astype(kind)


def setup_inputs(seed: int = 0) -> dict:
    keys = jax.random.split(jax.random.key(seed), 11)
    return {
        "head_ensemble": scatter_about(keys[0], (AQUIFER_LAYERS, MEMBERS, ROWS, COLS), 1.0, 6.0, ((2, 32), (3, 8)), jnp.float32),
        "transmissivity_grid": jnp.clip(jnp.exp(math.log(0.08) - 1.3862944 * jax.random.uniform(keys[1], (AQUIFER_LAYERS, ROWS, COLS), jnp.float32) ** levels(keys[1], (AQUIFER_LAYERS, ROWS, COLS), ((1, 32), (2, 8)), -0.2, 0.2)), 0.02, 0.08),
        "interlayer_leakage_factor": jnp.clip(jnp.exp(math.log(0.3) - 1.7917595 * jax.random.uniform(keys[2], (ROWS, COLS), jnp.float32) ** levels(keys[2], (ROWS, COLS), ((0, 32), (1, 8)), -0.2, 0.2)), 0.05, 0.3),
        "specific_porosity_release": jnp.clip(jnp.exp(math.log(1.5) - 1.60943787 * jax.random.uniform(keys[3], (ROWS, COLS), jnp.float32) ** levels(keys[3], (ROWS, COLS), ((0, 32), (1, 8)), -0.2, 0.2)), 0.3, 1.5),
        "infiltration_inflow": scatter_about(keys[4], (ROWS, COLS), 0.3, 1.8, ((0, 32), (1, 8)), jnp.float32),
        "obs_value": scatter_about(keys[5], (ANALYSES, BATCHES, LAT_ROWS, LAT_COLS), 1.5, 6.0, (), jnp.float32),
        "obs_error": jnp.clip(jnp.exp(jax.random.uniform(keys[6], (ANALYSES, BATCHES, LAT_ROWS, LAT_COLS), jnp.float32, math.log(0.1), math.log(1.0))), 0.1, 1.0),
        "obs_spot": set_ends(jax.random.randint(keys[7], (ANALYSES, BATCHES, LAT_ROWS, LAT_COLS), 0, SPAN * SPAN), jax.random.fold_in(keys[7], 1), 0, (SPAN * SPAN) - 1).astype(jnp.int32),
        "obs_live": draw_obs_live(jax.random.fold_in(keys[10], 71), 0),
        "batch_colour": draw_batch_colour(jax.random.fold_in(keys[10], 71), 0),
    }


STEP_SIZE = 0.5
STORAGE_FLOOR = 0.5
LOWER_WEIGHT = 0.6
TOP_LEVEL = lax.Precision.HIGHEST

def neighbours(field):
    padded = jnp.pad(field, ((0, 0), (0, 0), (1, 1), (1, 1)))
    return padded[:, :, 2:, 1:-1] + padded[:, :, :-2, 1:-1] + padded[:, :, 1:-1, 2:] + padded[:, :, 1:-1, :-2]

def advance(current, start, transmissivity_grid, interlayer_leakage_factor, specific_porosity_release, infiltration_inflow):
    lateral = transmissivity_grid[:, None] * (neighbours(current) - 4.0 * current)
    exchange_flow = interlayer_leakage_factor * (current[1] - current[0])
    vertical = jnp.stack([exchange_flow + infiltration_inflow, -exchange_flow])
    storage_term = specific_porosity_release * jax.nn.sigmoid(current) + STORAGE_FLOOR
    return start + STEP_SIZE * (lateral + vertical) / storage_term

def predicted_piezometric_ensemble(piezometric_elevation, transmissivity_grid, interlayer_leakage_factor, specific_porosity_release, infiltration_inflow):
    current = piezometric_elevation
    for step in range(ITERS):
        current = advance(current, piezometric_elevation, transmissivity_grid, interlayer_leakage_factor, specific_porosity_release, infiltration_inflow)
    return current

def analyse(piezometric_elevation, value_entries, errors, spots, lives, colours):
    margin = RADIUS - 1
    width = 2 * RADIUS - 1
    padded = jnp.pad(piezometric_elevation, ((0, 0), (0, 0), (margin, margin), (margin, margin)))
    offsets = (jnp.arange(width) - margin).astype(jnp.float32)
    taper = 1.0 - jnp.abs(offsets) / RADIUS
    window_weight = taper[:, None] * taper[None, :]
    layer_weight = jnp.array([1.0, LOWER_WEIGHT], jnp.float32)
    zero = jnp.zeros((), jnp.int32)
    for batch in range(BATCHES):
        colour = colours[batch].astype(jnp.int32)
        row_parity = colour // 2
        col_parity = colour % 2

        def visit(flat, state):
            lat_row = (flat // LAT_COLS).astype(jnp.int32)
            lat_col = (flat % LAT_COLS).astype(jnp.int32)
            spot = spots[batch, lat_row, lat_col].astype(jnp.int32)
            row = ((2 * lat_row + row_parity) * SPAN + spot // SPAN).astype(jnp.int32)
            col = ((2 * lat_col + col_parity) * SPAN + spot % SPAN).astype(jnp.int32)
            window = lax.dynamic_slice(state, (zero, zero, row, col), (AQUIFER_LAYERS, MEMBERS, width, width))
            prior = window[0, :, margin, margin]
            prior_mean = jnp.mean(prior)
            prior_anomaly = prior - prior_mean
            spread = jnp.sum(prior_anomaly * prior_anomaly) / (MEMBERS - 1)
            noise = errors[batch, lat_row, lat_col]
            live = lives[batch, lat_row, lat_col].astype(jnp.float32)
            gain = live / ((spread + noise) * (MEMBERS - 1))
            shrink = 1.0 / (1.0 + jnp.sqrt(noise / (spread + noise)))
            centre = lax.optimization_barrier(jnp.mean(window, axis=1, keepdims=True))
            deviation = window - centre
            moment_sum = jnp.einsum('lmrc,m->lrc', deviation, prior_anomaly, precision=TOP_LEVEL)
            weight = layer_weight[:, None, None] * window_weight[None] * gain * moment_sum
            innovation = value_entries[batch, lat_row, lat_col] - prior_mean
            result = centre + (weight * innovation)[:, None] + deviation - shrink * weight[:, None] * prior_anomaly[None, :, None, None]
            return lax.dynamic_update_slice(state, result, (zero, zero, row, col))
        padded = lax.fori_loop(0, LAT_ROWS * LAT_COLS, visit, padded)
    return padded[:, :, margin:margin + ROWS, margin:margin + COLS]

def reference(head_ensemble, transmissivity_grid, interlayer_leakage_factor, specific_porosity_release, infiltration_inflow, obs_value, obs_error, obs_spot, obs_live, batch_colour):
    piezometric_elevation = head_ensemble
    for analysis in range(ANALYSES):
        piezometric_elevation = predicted_piezometric_ensemble(piezometric_elevation, transmissivity_grid, interlayer_leakage_factor, specific_porosity_release, infiltration_inflow)
        piezometric_elevation = analyse(piezometric_elevation, obs_value[analysis], obs_error[analysis], obs_spot[analysis], obs_live[analysis], batch_colour[analysis])
    return piezometric_elevation
```

```python
import jax
import jax.numpy as jnp
from jax import lax
from jax.experimental import pallas as pl
from jax.experimental.pallas import tpu as pltpu
from jax.sharding import PartitionSpec as P

ITERS = 3
ANALYSES = 2
BATCHES = 4
MEMBERS = 64
RADIUS = 8
SPAN = 16
LOWER_WEIGHT = 0.6
LANES = 128

ROWS = 32
COLS = 128
HALO = 6
EDGE = 8
SKIRT = 3
EXT_ROWS = ROWS + 2 * HALO
EXT_COLS = COLS + 2 * EDGE
WIDE_COLS = EXT_COLS + 2 * EDGE
SIDE = 24
PAD_ROWS = 80
PAD_COLS = 184
CELL_ROWS = 6
CELL_COLS = 12
SLOTS = CELL_ROWS * CELL_COLS
OWN_ROWS = 2
OWN_COLS = 8
OWN = OWN_ROWS * OWN_COLS
KINDS = 8
WINDOW = 2 * RADIUS - 1

F32 = jnp.float32
BF16 = jnp.bfloat16
SMEM = pl.BlockSpec(memory_space=pltpu.SMEM)
VMEM = pl.BlockSpec(memory_space=pltpu.VMEM)
HBM = pl.BlockSpec(memory_space=pl.ANY)


def params():
    return pltpu.CompilerParams(vmem_limit_bytes=56 * 2**20)


def turn_kernel(place, heads, coefs, turned, tiles, give_even, give_odd):
    def body(row, carry):
        turned[row] = heads[pl.ds(row, LANES, stride=ROWS), :].T
        return carry

    lax.fori_loop(0, ROWS, body, 0, unroll=4)
    for half in range(2):
        tiles[half] = coefs[half].T
    odd = place[0]
    even_from = (1 - odd) * (ROWS - HALO)
    odd_from = odd * (ROWS - HALO)
    give_even[0:HALO] = turned[pl.ds(even_from, HALO)]
    give_odd[0:HALO] = turned[pl.ds(odd_from, HALO)]
    give_even[HALO] = tiles[1 - odd]
    give_odd[HALO] = tiles[odd]


def turn(place, heads, coefs):
    return pl.pallas_call(
        turn_kernel,
        out_shape=(
            jax.ShapeDtypeStruct((ROWS, COLS, LANES), F32),
            jax.ShapeDtypeStruct((2, COLS, LANES), F32),
            jax.ShapeDtypeStruct((HALO + 1, COLS, LANES), F32),
            jax.ShapeDtypeStruct((HALO + 1, COLS, LANES), F32),
        ),
        in_specs=[SMEM, VMEM, VMEM],
        out_specs=(VMEM, VMEM, VMEM, VMEM),
        compiler_params=params(),
        name="turn",
    )(place, heads, coefs)


def strip_kernel(place, left, right, tiles_left, tiles_right, even_left, even_right, odd_left, odd_right, give_even, give_odd):
    def strip(inner, tiles, even, odd):
        south = jnp.where(place[0] == 0, even[...], odd[...])
        north = jnp.where(place[0] == 0, odd[...], even[...])
        return jnp.concatenate(
            [north[:HALO], inner[...], south[:HALO], north[HALO:], tiles[...], south[HALO:]], axis=0
        )

    west = strip(left, tiles_left, even_left, odd_left)
    east = strip(right, tiles_right, even_right, odd_right)
    give_even[...] = jnp.where(place[1] == 0, east, west)
    give_odd[...] = jnp.where(place[1] == 0, west, east)


def strips(place, turned, tiles, got_even, got_odd):
    last = COLS // EDGE - 1

    def cut(depth, at):
        return pl.BlockSpec((depth, EDGE, LANES), lambda i: (0, at, 0))

    whole = pl.BlockSpec((EXT_ROWS + 4, EDGE, LANES), lambda i: (0, 0, 0))
    shape = jax.ShapeDtypeStruct((EXT_ROWS + 4, EDGE, LANES), F32)
    return pl.pallas_call(
        strip_kernel,
        grid=(1,),
        out_shape=(shape, shape),
        in_specs=[
            SMEM,
            cut(ROWS, 0),
            cut(ROWS, last),
            cut(2, 0),
            cut(2, last),
            cut(HALO + 1, 0),
            cut(HALO + 1, last),
            cut(HALO + 1, 0),
            cut(HALO + 1, last),
        ],
        out_specs=(whole, whole),
        compiler_params=params(),
        name="strips",
    )(place, turned, turned, tiles, tiles, got_even, got_even, got_odd, got_odd)


def spread_matrix():
    lane = lax.broadcasted_iota(jnp.int32, (2 * LANES, 4 * LANES), 0) % KINDS
    out = lax.broadcasted_iota(jnp.int32, (2 * LANES, 4 * LANES), 1)
    group = out // LANES
    lower = out % LANES >= MEMBERS
    wanted = jnp.where(group == 0, jnp.where(lower, 1, 0), group + 1)
    wanted = jnp.where((group == 3) & lower, KINDS, wanted)
    return (lane == wanted).astype(BF16)


def spread_coefs(tiles, coef, first, count):
    matrix = spread_matrix()
    owner = lax.broadcasted_iota(jnp.int32, (EXT_COLS, LANES), 1) // KINDS

    def body(step, carry):
        row = step + first + SPAN
        tile = jnp.where(owner == row % SPAN, tiles[row // SPAN], 0.0)
        high = tile.astype(BF16)
        low = (tile - high.astype(F32)).astype(BF16)
        wide = jnp.dot(jnp.concatenate([high, low], axis=1), matrix, preferred_element_type=F32)
        for kind in range(4):
            coef[kind, step] = wide[:, kind * LANES : (kind + 1) * LANES]
        return carry

    lax.fori_loop(0, count, body, 0, unroll=2)


def storage_step(src, src_at, start, start_at, dst, dst_at, coef, coef_at, low, high, col, width):
    def body(row, carry):
        def read(ref, at, dr, dc):
            return ref[row + (at[0] + dr), at[1] + col + dc : at[1] + col + dc + width, :]

        def factor(kind):
            return coef[kind, row + coef_at, EDGE + col : EDGE + col + width, :]

        u = read(src, src_at, 0, 0)
        around = read(src, src_at, -1, 0) + read(src, src_at, 1, 0) + read(src, src_at, 0, -1) + read(src, src_at, 0, 1)
        exchange = pltpu.roll(u, MEMBERS, 1) - u
        top = factor(0) * (around - 4.0 * u) + factor(1) * exchange + factor(3)
        bottom = factor(2) * (1.0 + jnp.tanh(0.5 * u)) + 1.0
        value = read(start, start_at, 0, 0) + top / bottom
        dst[row + dst_at[0], dst_at[1] + col : dst_at[1] + col + width, :] = value
        return carry

    lax.fori_loop(low, high, body, 0, unroll=4 if (high - low) % 4 == 0 else 2)


def pick_slots(src, at, rows, cols, out):
    for slot in range(OWN):
        cell = (2 + slot // OWN_COLS) * CELL_COLS + 2 + slot % OWN_COLS
        out[slot : slot + 1, :] = src[rows[cell] + at[0], pl.ds(cols[cell] + at[1], 1), :]


def first_kernel(place, rows, cols, turned, tiles, ns_even, ns_odd, ew_even, ew_odd, cast, slots, ext_tiles, start, one, two, coef):
    odd_n, odd_e = place[0], place[1]
    inner = pl.ds(2 * EDGE, COLS)
    even_row = (1 - odd_n) * (ROWS + HALO)
    odd_row = odd_n * (ROWS + HALO)
    start[HALO : HALO + ROWS, inner, :] = turned[...]
    start[pl.ds(even_row, HALO), inner, :] = ns_even[:HALO]
    start[pl.ds(odd_row, HALO), inner, :] = ns_odd[:HALO]
    even_col = pl.multiple_of(EDGE + (1 - odd_e) * (COLS + EDGE), EDGE)
    odd_col = pl.multiple_of(EDGE + odd_e * (COLS + EDGE), EDGE)
    start[:, pl.ds(even_col, EDGE), :] = ew_even[:EXT_ROWS]
    start[:, pl.ds(odd_col, EDGE), :] = ew_odd[:EXT_ROWS]
    ext_tiles[1:3, EDGE : EDGE + COLS, :] = tiles[...]
    ext_tiles[(1 - odd_n) * 3, EDGE : EDGE + COLS, :] = ns_even[HALO]
    ext_tiles[odd_n * 3, EDGE : EDGE + COLS, :] = ns_odd[HALO]
    ext_tiles[:, pl.ds(pl.multiple_of(even_col - EDGE, EDGE), EDGE), :] = ew_even[EXT_ROWS:]
    ext_tiles[:, pl.ds(pl.multiple_of(odd_col - EDGE, EDGE), EDGE), :] = ew_odd[EXT_ROWS:]
    spread_coefs(ext_tiles, coef, -HALO, EXT_ROWS)
    at = (HALO, 2 * EDGE)
    storage_step(start, at, start, at, one, at, coef, HALO, -5, ROWS + 5, -EDGE, EXT_COLS)
    storage_step(one, at, start, at, two, at, coef, HALO, -4, ROWS + 4, -EDGE, EXT_COLS)
    out_at = (SKIRT, EDGE)
    storage_step(two, at, start, at, cast, out_at, coef, HALO, -SKIRT, ROWS + SKIRT, -EDGE, EXT_COLS)
    pick_slots(cast, out_at, rows, cols, slots)


def first_forecast(place, rows, cols, turned, tiles, ns_even, ns_odd, ew_even, ew_odd):
    return pl.pallas_call(
        first_kernel,
        out_shape=(
            jax.ShapeDtypeStruct((ROWS + 2 * SKIRT, EXT_COLS, LANES), F32),
            jax.ShapeDtypeStruct((OWN, LANES), F32),
            jax.ShapeDtypeStruct((4, EXT_COLS, LANES), F32),
        ),
        in_specs=[SMEM, SMEM, SMEM] + [VMEM] * 6,
        out_specs=(VMEM, VMEM, VMEM),
        scratch_shapes=[pltpu.VMEM((EXT_ROWS, WIDE_COLS, LANES), F32)] * 3
        + [pltpu.VMEM((4, EXT_ROWS, EXT_COLS, LANES), F32)],
        compiler_params=params(),
        name="first_forecast",
    )(place, rows, cols, turned, tiles, ns_even, ns_odd, ew_even, ew_odd)


def serial_slots(place, mid, got_even, got_odd, table, across, members, anomaly, change):
    odd = place[0] == 1
    south = jnp.where(odd, got_odd[...], got_even[...])
    north = jnp.where(odd, got_even[...], got_odd[...])
    for third, source in enumerate((north, mid[...], south)):
        for half in range(OWN_ROWS):
            base = (third * OWN_ROWS + half) * CELL_COLS
            own = half * OWN_COLS
            members[base : base + 2, :] = source[own + OWN_COLS - 2 : own + OWN_COLS]
            members[base + 2 : base + 2 + OWN_COLS, :] = source[OWN + own : OWN + own + OWN_COLS]
            members[base + 2 + OWN_COLS : base + CELL_COLS, :] = source[2 * OWN + own : 2 * OWN + own + 2]
    lane = lax.broadcasted_iota(jnp.int32, (SLOTS, LANES), 1)
    prior = members[...]
    prior = jnp.where(lane < MEMBERS, prior, pltpu.roll(prior, MEMBERS, 1))
    value, noise, live = table[:, 0:1], table[:, 1:2], table[:, 2:3]
    near = jnp.maximum(0.0, 1.0 - jnp.abs(table[:, 3:4] - across[3:4, :]) / RADIUS)
    near = near * jnp.maximum(0.0, 1.0 - jnp.abs(table[:, 4:5] - across[4:5, :]) / RADIUS)
    turn_of = table[:, 5:6]
    kept_anomaly = jnp.zeros((SLOTS, LANES), F32)
    kept_change = jnp.zeros((SLOTS, LANES), F32)
    for batch in range(BATCHES):
        now = turn_of == float(batch)
        mean = jnp.sum(prior, axis=1, keepdims=True) / LANES
        off = prior - mean
        spread = jnp.sum(off * off, axis=1, keepdims=True) / (2.0 * (MEMBERS - 1))
        gain = live / ((spread + noise) * (MEMBERS - 1))
        shrink = 1.0 / (1.0 + jnp.sqrt(noise / (spread + noise)))
        delta = jnp.where(now, gain * ((value - mean) - shrink * off), 0.0)
        kept_anomaly = jnp.where(now, off, kept_anomaly)
        kept_change = jnp.where(now, delta, kept_change)
        if batch < BATCHES - 1:
            cross = lax.dot_general(
                prior, off, (((1,), (1,)), ((), ())), precision=lax.Precision.HIGHEST, preferred_element_type=F32
            )
            prior = prior + jnp.dot(
                0.5 * near * cross, delta, precision=lax.Precision.HIGHEST, preferred_element_type=F32
            )
    anomaly[...] = kept_anomaly
    change[...] = kept_change


def windows(rows, cols, live, colours, state, anomaly, change, skirt):
    lane_in = lax.broadcasted_iota(jnp.int32, (2 * LANES, LANES), 0) % LANES
    lane_out = lax.broadcasted_iota(jnp.int32, (2 * LANES, LANES), 1)
    ones = ((lane_in // MEMBERS) == (lane_out // MEMBERS)).astype(BF16)
    offset = lax.broadcasted_iota(jnp.int32, (2 * RADIUS, LANES), 0) - (RADIUS - 1)
    lane = lax.broadcasted_iota(jnp.int32, (2 * RADIUS, LANES), 1)
    taper = jnp.maximum(0.0, 1.0 - jnp.abs(offset).astype(F32) / RADIUS)
    taper = taper * jnp.where(lane < MEMBERS, 1.0, LOWER_WEIGHT)
    count = CELL_COLS // 2 - 1
    shift = SIDE - (RADIUS - 1)

    def group(step, carry):
        colour = colours[step // 2]
        down = colour // 2
        right = colour % 2
        cell_row = 2 - down + 2 * (step % 2)
        first = cell_row * CELL_COLS + 2 - right
        cells = [first + 2 * i for i in range(count)]
        wanted = jnp.zeros((), jnp.bool_)
        for cell in cells:
            meets = (rows[cell] + RADIUS > -skirt) & (rows[cell] - RADIUS < ROWS - 1 + skirt)
            wanted = wanted | (meets & (live[cell] != 0))

        @pl.when(wanted)
        def _():
            held, products = [], []
            for cell in cells:
                row, col = rows[cell] + shift, cols[cell] + shift
                pattern = anomaly[pl.ds(cell, 1), :]
                for i in range(WINDOW):
                    x = state[row + i, pl.ds(col, 2 * RADIUS), :]
                    held.append(x)
                    products.append(x * pattern)
            product = jnp.concatenate(products, axis=0)
            high = product.astype(BF16)
            low = (product - high.astype(F32)).astype(BF16)
            moment = jnp.dot(jnp.concatenate([high, low], axis=1), ones, preferred_element_type=F32)
            for n, cell in enumerate(cells):
                row, col = rows[cell] + shift, cols[cell] + shift
                delta = change[pl.ds(cell, 1), :]
                for i in range(WINDOW):
                    at = n * WINDOW + i
                    weight = taper * (1.0 - abs(i - (RADIUS - 1)) / RADIUS)
                    part = moment[at * 2 * RADIUS : (at + 1) * 2 * RADIUS]
                    state[row + i, pl.ds(col, 2 * RADIUS), :] = held[at] + part * weight * delta

        return carry

    lax.fori_loop(0, 2 * BATCHES, group, 0)


def middle_kernel(
    place, rows, cols, live, colours, next_rows, next_cols, table, across, mid, got_even, got_odd, ext_tiles, cast,
    result, slots, state, members, anomaly, change, one, two, coef, arrived,
):
    copy = pltpu.make_async_copy(
        cast, state.at[pl.ds(SIDE - SKIRT, ROWS + 2 * SKIRT), pl.ds(SIDE - EDGE, EXT_COLS), :], arrived
    )
    copy.start()
    serial_slots(place, mid, got_even, got_odd, table, across, members, anomaly, change)
    spread_coefs(ext_tiles, coef, -SKIRT, ROWS + 2 * SKIRT)
    copy.wait()
    windows(rows, cols, live, colours, state, anomaly, change, SKIRT)
    big = (SIDE, SIDE)
    at = (SKIRT, 2 * EDGE)
    storage_step(state, big, state, big, one, at, coef, SKIRT, -2, ROWS + 2, -EDGE, EXT_COLS)
    storage_step(one, at, state, big, two, at, coef, SKIRT, -1, ROWS + 1, -EDGE, EXT_COLS)
    storage_step(two, at, state, big, result, (0, 0), coef, SKIRT, 0, ROWS, 0, COLS)
    pick_slots(result, (0, 0), next_rows, next_cols, slots)


def middle(place, rows, cols, live, colours, next_rows, next_cols, table, across, mid, got_even, got_odd, ext_tiles, cast):
    return pl.pallas_call(
        middle_kernel,
        out_shape=(
            jax.ShapeDtypeStruct((ROWS, COLS, LANES), F32),
            jax.ShapeDtypeStruct((OWN, LANES), F32),
        ),
        in_specs=[SMEM] * 7 + [VMEM] * 6 + [HBM],
        out_specs=(VMEM, VMEM),
        scratch_shapes=[pltpu.VMEM((PAD_ROWS, PAD_COLS, LANES), F32)]
        + [pltpu.VMEM((SLOTS, LANES), F32)] * 3
        + [pltpu.VMEM((ROWS + 2 * SKIRT, WIDE_COLS, LANES), F32)] * 2
        + [pltpu.VMEM((4, ROWS + 2 * SKIRT, EXT_COLS, LANES), F32), pltpu.SemaphoreType.DMA(())],
        compiler_params=params(),
        name="middle",
    )(place, rows, cols, live, colours, next_rows, next_cols, table, across, mid, got_even, got_odd, ext_tiles, cast)


def last_kernel(
    place, rows, cols, live, colours, table, across, mid, got_even, got_odd, cast, heads, state, members, anomaly, change, arrived
):
    copy = pltpu.make_async_copy(cast, state.at[pl.ds(SIDE, ROWS), pl.ds(SIDE, COLS), :], arrived)
    copy.start()
    serial_slots(place, mid, got_even, got_odd, table, across, members, anomaly, change)
    copy.wait()
    windows(rows, cols, live, colours, state, anomaly, change, 0)

    def body(row, carry):
        heads[pl.ds(row, LANES, stride=ROWS), :] = state[row + SIDE, SIDE : SIDE + COLS, :].T
        return carry

    lax.fori_loop(0, ROWS, body, 0, unroll=4)


def last(place, rows, cols, live, colours, table, across, mid, got_even, got_odd, cast):
    return pl.pallas_call(
        last_kernel,
        out_shape=jax.ShapeDtypeStruct((LANES * ROWS, COLS), F32),
        in_specs=[SMEM] * 5 + [VMEM] * 5 + [HBM],
        out_specs=VMEM,
        scratch_shapes=[pltpu.VMEM((PAD_ROWS, PAD_COLS, LANES), F32)]
        + [pltpu.VMEM((SLOTS, LANES), F32)] * 3
        + [pltpu.SemaphoreType.DMA(())],
        compiler_params=params(),
        name="last",
    )(place, rows, cols, live, colours, table, across, mid, got_even, got_odd, cast)


def swap(x, axis, odd):
    peers = lax.axis_size(axis)
    low = range(odd, peers - 1, 2)
    return lax.ppermute(x, axis, [(i, i + 1) for i in low] + [(i + 1, i) for i in low])


def gather_slots(slots, odd_e):
    even = swap(slots, "east", 0)
    odd = swap(slots, "east", 1)
    west = jnp.where(odd_e == 0, odd, even)
    east = jnp.where(odd_e == 0, even, odd)
    mid = jnp.concatenate([west, slots, east], axis=0)
    return mid, swap(mid, "north", 0), swap(mid, "north", 1)


def slot_tables(obs_value, obs_error, obs_spot, obs_live, batch_colour, north_at, east_at):
    margins = ((0, 0), (0, 0), (1, 1), (1, 1))
    lat_cols = COLS // (2 * SPAN)
    stacked = jnp.stack(
        [
            jnp.pad(obs_value, margins),
            jnp.pad(obs_error, margins, constant_values=1.0),
            jnp.pad(obs_spot, margins).astype(F32),
            jnp.pad(obs_live, margins).astype(F32),
        ]
    )
    near = lax.dynamic_slice(
        stacked, (0, 0, 0, north_at, east_at * lat_cols), (4, ANALYSES, BATCHES, CELL_ROWS // 2, CELL_COLS // 2)
    )
    is_colour = batch_colour[:, None, :] == jnp.arange(4)[None, :, None]
    coloured = jnp.sum(jnp.where(is_colour[None, :, :, :, None, None], near[:, :, None], 0.0), axis=3)
    coloured = coloured.reshape(4, ANALYSES, 2, 2, CELL_ROWS // 2, CELL_COLS // 2)
    grid = coloured.transpose(0, 1, 4, 2, 5, 3).reshape(4, ANALYSES, CELL_ROWS, CELL_COLS)
    value, noise, spot, live = grid
    spot = spot.astype(jnp.int32)
    cell_row = jnp.arange(CELL_ROWS)[:, None]
    cell_col = jnp.arange(CELL_COLS)[None, :]
    row = (cell_row - 2) * SPAN + spot // SPAN
    col = (cell_col - 2) * SPAN + spot % SPAN
    turns = jnp.sum(jnp.where(is_colour, jnp.arange(BATCHES)[None, None, :], 0), axis=2)
    turns = turns.reshape(ANALYSES, 2, 2)
    turns = jnp.tile(turns, (1, CELL_ROWS // 2, CELL_COLS // 2))
    fields = jnp.stack(
        [value, noise, live, row.astype(F32), col.astype(F32), turns.astype(F32), live, live], axis=1
    ).reshape(ANALYSES, 8, SLOTS)
    flat = (ANALYSES, SLOTS)
    return (
        fields,
        fields.transpose(0, 2, 1),
        row.reshape(flat).astype(jnp.int32),
        col.reshape(flat).astype(jnp.int32),
        live.reshape(flat).astype(jnp.int32),
    )


def shards(
    head_ensemble,
    transmissivity_grid,
    interlayer_leakage_factor,
    specific_porosity_release,
    infiltration_inflow,
    obs_value,
    obs_error,
    obs_spot,
    obs_live,
    batch_colour,
):
    north_at = lax.axis_index("north")
    east_at = lax.axis_index("east")
    odd_n = north_at % 2
    odd_e = east_at % 2
    place = jnp.stack([odd_n, odd_e]).astype(jnp.int32)
    zero = jnp.zeros((ROWS, COLS), F32)
    coefs = jnp.stack(
        [
            transmissivity_grid[0],
            transmissivity_grid[1],
            interlayer_leakage_factor,
            specific_porosity_release,
            infiltration_inflow,
            zero,
            zero,
            zero,
        ],
        axis=1,
    ).reshape(2, LANES, COLS)
    across, table, rows, cols, live = slot_tables(
        obs_value, obs_error, obs_spot, obs_live, batch_colour, north_at, east_at
    )
    colours = batch_colour.astype(jnp.int32)

    turned, tiles, give_even, give_odd = turn(place, head_ensemble.reshape(LANES * ROWS, COLS), coefs)
    ns_even = swap(give_even, "north", 0)
    ns_odd = swap(give_odd, "north", 1)
    give_even, give_odd = strips(place, turned, tiles, ns_even, ns_odd)
    ew_even = swap(give_even, "east", 0)
    ew_odd = swap(give_odd, "east", 1)
    cast, slots, ext_tiles = first_forecast(
        place, rows[0], cols[0], turned, tiles, ns_even, ns_odd, ew_even, ew_odd
    )
    mid, got_even, got_odd = gather_slots(slots, odd_e)
    cast, slots = middle(
        place, rows[0], cols[0], live[0], colours[0], rows[1], cols[1], table[0], across[0], mid, got_even, got_odd,
        ext_tiles, cast,
    )
    mid, got_even, got_odd = gather_slots(slots, odd_e)
    heads = last(
        place, rows[1], cols[1], live[1], colours[1], table[1], across[1], mid, got_even, got_odd, cast
    )
    return heads.reshape(2, MEMBERS, ROWS, COLS)


def solution(mesh):
    placed = (
        P(None, None, "north", "east"),
        P(None, "north", "east"),
        P("north", "east"),
        P("north", "east"),
        P("north", "east"),
        P(),
        P(),
        P(),
        P(),
        P(),
    )
    return jax.shard_map(
        shards,
        mesh=mesh,
        in_specs=placed,
        out_specs=P(None, None, "north", "east"),
        check_vma=False,
    )
```

```python
import jax
import jax.numpy as jnp
from jax import lax
from jax.experimental import pallas as pl
from jax.experimental.pallas import tpu as pltpu
from jax.sharding import PartitionSpec as P

ITERS = 3
ANALYSES = 2
BATCHES = 4
MEMBERS = 64
RADIUS = 8
SPAN = 16
LOWER_WEIGHT = 0.6
LANES = 128

ROWS = 32
COLS = 128
HALO = 6
EDGE = 8
SKIRT = 3
EXT_ROWS = ROWS + 2 * HALO
EXT_COLS = COLS + 2 * EDGE
WIDE_COLS = EXT_COLS + 2 * EDGE
SIDE = 24
PAD_ROWS = 80
PAD_COLS = 184
CELL_ROWS = 6
CELL_COLS = 12
SLOTS = CELL_ROWS * CELL_COLS
OWN_ROWS = 2
OWN_COLS = 8
OWN = OWN_ROWS * OWN_COLS
KINDS = 8
WINDOW = 2 * RADIUS - 1

VMEM_BYTES = 64 * 2**20

F32 = jnp.float32
BF16 = jnp.bfloat16
SMEM = pl.BlockSpec(memory_space=pltpu.SMEM)
VMEM = pl.BlockSpec(memory_space=pltpu.VMEM)
HBM = pl.BlockSpec(memory_space=pl.ANY)
MARKS = pltpu.SMEM((8, LANES), jnp.int32)


def params():
    return pltpu.CompilerParams(vmem_limit_bytes=VMEM_BYTES)


def weight(microseconds):
    return pl.CostEstimate(flops=0, bytes_accessed=int(microseconds * 3.5e6), transcendentals=0)


def parity(axis):
    return lax.axis_index(axis) % 2


def edge_kernel(top, bottom, transmissivity, leakage, release, inflow, tiles, give_even, give_odd, stacked):
    stacked[...] = jnp.zeros_like(stacked)
    for half in range(2):
        part = slice(half * SPAN, (half + 1) * SPAN)
        for kind, field in enumerate((transmissivity.at[0], transmissivity.at[1], leakage, release, inflow)):
            stacked[pl.ds(half * LANES + kind, SPAN, stride=KINDS), :] = field[part, :]
        tiles[half] = stacked[half * LANES : (half + 1) * LANES, :].T
    odd = parity("north")
    for row in range(HALO):
        upper = top[pl.ds(row, LANES, stride=8), :].T
        lower = bottom[pl.ds(8 - HALO + row, LANES, stride=8), :].T
        give_even[row] = jnp.where(odd == 0, lower, upper)
        give_odd[row] = jnp.where(odd == 0, upper, lower)
    give_even[HALO] = tiles[1 - odd]
    give_odd[HALO] = tiles[odd]


def edges(heads, transmissivity, leakage, release, inflow):
    def rows_at(at):
        return pl.BlockSpec((LANES, 8, COLS), lambda i: (0, at, 0))

    def kernel(top, bottom, *rest):
        edge_kernel(top.reshape(LANES * 8, COLS), bottom.reshape(LANES * 8, COLS), *rest)

    halo = jax.ShapeDtypeStruct((HALO + 1, COLS, LANES), F32)
    return pl.pallas_call(
        kernel,
        grid=(1,),
        out_shape=(jax.ShapeDtypeStruct((2, COLS, LANES), F32), halo, halo),
        in_specs=[rows_at(0), rows_at(ROWS // 8 - 1)] + [VMEM] * 4,
        out_specs=(VMEM, VMEM, VMEM),
        scratch_shapes=[pltpu.VMEM((2 * LANES, COLS), F32)],
        compiler_params=params(),
        name="edges",
    )(heads, heads, transmissivity, leakage, release, inflow)


def turn_kernel(heads, tiles, turned, give_even, give_odd):
    def body(row, carry):
        turned[row] = heads[pl.ds(row, LANES, stride=ROWS), :].T
        return carry

    lax.fori_loop(0, ROWS, body, 0, unroll=16)
    odd = parity("east")
    for give, at in ((give_even, 1 - odd), (give_odd, odd)):
        cols = pl.ds(pl.multiple_of(at * (COLS - EDGE), EDGE), EDGE)
        give[:ROWS] = turned[:, cols, :]
        give[ROWS:] = tiles[:, cols, :]


def turn(heads, tiles):
    strip = jax.ShapeDtypeStruct((ROWS + 2, EDGE, LANES), F32)
    return pl.pallas_call(
        turn_kernel,
        out_shape=(jax.ShapeDtypeStruct((ROWS, COLS, LANES), F32), strip, strip),
        in_specs=[VMEM, VMEM],
        out_specs=(VMEM, VMEM, VMEM),
        compiler_params=params(),
        cost_estimate=weight(4),
        name="turn",
    )(heads, tiles)


def corner_kernel(even_left, even_right, odd_left, odd_right, give_even, give_odd):
    flip_n = parity("north") == 0
    flip_e = parity("east") == 0
    for half, swap_n in enumerate((flip_n, jnp.logical_not(flip_n))):
        left = jnp.where(swap_n, odd_left[...], even_left[...])
        right = jnp.where(swap_n, odd_right[...], even_right[...])
        part = slice(half * (HALO + 1), (half + 1) * (HALO + 1))
        give_even[part] = jnp.where(flip_e, right, left)
        give_odd[part] = jnp.where(flip_e, left, right)


def corners(got_even, got_odd):
    def cut(at):
        return pl.BlockSpec((HALO + 1, EDGE, LANES), lambda i: (0, at, 0))

    last = COLS // EDGE - 1
    whole = pl.BlockSpec((2 * HALO + 2, EDGE, LANES), lambda i: (0, 0, 0))
    shape = jax.ShapeDtypeStruct((2 * HALO + 2, EDGE, LANES), F32)
    return pl.pallas_call(
        corner_kernel,
        grid=(1,),
        out_shape=(shape, shape),
        in_specs=[cut(0), cut(last), cut(0), cut(last)],
        out_specs=(whole, whole),
        compiler_params=params(),
        name="corners",
    )(got_even, got_even, got_odd, got_odd)


def spread_matrix():
    lane = lax.broadcasted_iota(jnp.int32, (2 * LANES, 4 * LANES), 0) % KINDS
    out = lax.broadcasted_iota(jnp.int32, (2 * LANES, 4 * LANES), 1)
    group = out // LANES
    lower = out % LANES >= MEMBERS
    wanted = jnp.where(group == 0, jnp.where(lower, 1, 0), group + 1)
    wanted = jnp.where((group == 3) & lower, KINDS, wanted)
    return (lane == wanted).astype(BF16)


def spread_rows(tiles, coef, matrix, first, rows):
    owner = lax.broadcasted_iota(jnp.int32, (EXT_COLS, LANES), 1) // KINDS
    parts = []
    for row in rows:
        parts.append(jnp.where(owner == (row + SPAN) % SPAN, tiles[(row + SPAN) // SPAN], 0.0))
    tile = jnp.concatenate(parts, axis=0)
    high = tile.astype(BF16)
    low = (tile - high.astype(F32)).astype(BF16)
    wide = jnp.dot(jnp.concatenate([high, low], axis=1), matrix, preferred_element_type=F32)
    for i, row in enumerate(rows):
        for kind in range(4):
            coef[kind, row - first] = wide[i * EXT_COLS : (i + 1) * EXT_COLS, kind * LANES : (kind + 1) * LANES]


def storage(u, around, start, factors):
    lateral, leakage, release, inflow = factors
    exchange = pltpu.roll(u, MEMBERS, 1) - u
    top = lateral * (around - 4.0 * u) + leakage * exchange + inflow
    bottom = release * (1.0 + jnp.tanh(0.5 * u)) + 1.0
    return start + top * pltpu.reciprocal(bottom, approx=True)


def storage_step(src, src_at, start, start_at, dst, dst_at, coef, coef_at, low, high, first, count, unroll=None):
    def strip(tile, carry):
        col = tile * 8 if unroll is None else pl.multiple_of(tile * 8, 8)

        def read(ref, at, row, shift=0):
            return ref[row + at[0], pl.ds(at[1] + 8 * first + shift + col, 8), :]

        above, u = read(src, src_at, low - 1), read(src, src_at, low)
        for row in range(low, high):
            below = read(src, src_at, row + 1)
            around = (above + below) + (read(src, src_at, row, -1) + read(src, src_at, row, 1))
            held = u if start is None else read(start, start_at, row)
            factors = [coef[kind, row + coef_at, pl.ds(EDGE + 8 * first + col, 8), :] for kind in range(4)]
            dst[row + dst_at[0], pl.ds(dst_at[1] + 8 * first + col, 8), :] = storage(u, around, held, factors)
            above, u = u, below
        return carry

    if unroll is None:
        for tile in range(count):
            strip(tile, 0)
    else:
        lax.fori_loop(0, count, strip, 0, unroll=unroll)


def fetch(pairs, sems):
    copies = [pltpu.make_async_copy(a, b, sems.at[i]) for i, (a, b) in enumerate(pairs)]
    for copy in copies:
        copy.start()
    return copies


def wait_for(copies):
    for copy in copies:
        copy.wait()


def first_kernel(
    turned, tiles, ns_even, ns_odd, ew_even, ew_odd, corner_even, corner_odd, marks_in,
    cast, slots, ext_tiles, start, one, two, coef, marks, tile_sems, sems,
):
    odd_n, odd_e = parity("north"), parity("east")
    even_row = (1 - odd_n) * (ROWS + HALO)
    odd_row = odd_n * (ROWS + HALO)
    even_col = (1 - odd_e) * (COLS + EDGE)
    odd_col = odd_e * (COLS + EDGE)
    inner = pl.ds(2 * EDGE, COLS)
    tile_inner = pl.ds(EDGE, COLS)
    moves = [
        (turned, start.at[pl.ds(HALO, ROWS), inner, :]),
        (ns_even.at[pl.ds(0, HALO)], start.at[pl.ds(even_row, HALO), inner, :]),
        (ns_odd.at[pl.ds(0, HALO)], start.at[pl.ds(odd_row, HALO), inner, :]),
    ]
    tile_moves = [
        (tiles, ext_tiles.at[pl.ds(1, 2), tile_inner, :]),
        (ns_even.at[pl.ds(HALO, 1)], ext_tiles.at[pl.ds((1 - odd_n) * 3, 1), tile_inner, :]),
        (ns_odd.at[pl.ds(HALO, 1)], ext_tiles.at[pl.ds(odd_n * 3, 1), tile_inner, :]),
    ]
    for at, strip, corner in ((even_col, ew_even, corner_even), (odd_col, ew_odd, corner_odd)):
        outer = pl.ds(pl.multiple_of(at + EDGE, EDGE), EDGE)
        tile_outer = pl.ds(pl.multiple_of(at, EDGE), EDGE)
        moves += [
            (strip.at[pl.ds(0, ROWS)], start.at[pl.ds(HALO, ROWS), outer, :]),
            (corner.at[pl.ds(0, HALO)], start.at[pl.ds(0, HALO), outer, :]),
            (corner.at[pl.ds(HALO + 1, HALO)], start.at[pl.ds(HALO + ROWS, HALO), outer, :]),
        ]
        tile_moves += [
            (strip.at[pl.ds(ROWS, 2)], ext_tiles.at[pl.ds(1, 2), tile_outer, :]),
            (corner.at[pl.ds(HALO, 1)], ext_tiles.at[pl.ds(0, 1), tile_outer, :]),
            (corner.at[pl.ds(2 * HALO + 1, 1)], ext_tiles.at[pl.ds(3, 1), tile_outer, :]),
        ]
    tile_copies = fetch(tile_moves, tile_sems)
    copies = fetch(moves + [(marks_in, marks)], sems)
    matrix = spread_matrix()
    wait_for(tile_copies)
    for part in range(4):
        spread_rows(ext_tiles, coef, matrix, -HALO, range(-HALO + part * 11, -HALO + part * 11 + 11))
    wait_for(copies)
    at = (HALO, 2 * EDGE)
    count = EXT_COLS // 8
    storage_step(start, at, None, at, one, at, coef, HALO, -5, ROWS + 5, -1, count, 9)
    storage_step(one, at, start, at, two, at, coef, HALO, -4, ROWS + 4, -1, count, 9)
    copies = []
    for part in range(3):
        first = -1 + part * count // 3
        storage_step(two, at, start, at, one, at, coef, HALO, -SKIRT, ROWS + SKIRT, first, count // 3, 6)
        copy = pltpu.make_async_copy(
            one.at[pl.ds(HALO - SKIRT, ROWS + 2 * SKIRT), pl.ds(2 * EDGE + 8 * first, 8 * count // 3), :],
            cast.at[:, pl.ds(EDGE + 8 * first, 8 * count // 3), :],
            sems.at[part],
        )
        copy.start()
        copies.append(copy)
    pick_slots(one, at, marks, 0, slots)
    wait_for(copies)


def first_forecast(pieces, marks):
    return pl.pallas_call(
        first_kernel,
        out_shape=(
            jax.ShapeDtypeStruct((ROWS + 2 * SKIRT, EXT_COLS, LANES), F32),
            jax.ShapeDtypeStruct((OWN, LANES), F32),
            jax.ShapeDtypeStruct((4, EXT_COLS, LANES), F32),
        ),
        in_specs=[HBM] * 9,
        out_specs=(HBM, VMEM, VMEM),
        scratch_shapes=[pltpu.VMEM((EXT_ROWS, WIDE_COLS, LANES), F32)] * 3
        + [pltpu.VMEM((4, EXT_ROWS, EXT_COLS, LANES), F32)]
        + [MARKS, pltpu.SemaphoreType.DMA((9,)), pltpu.SemaphoreType.DMA((10,))],
        compiler_params=params(),
        name="first_forecast",
    )(*pieces, marks)


def pick_slots(src, at, marks, cycle, out):
    for slot in range(OWN):
        cell = (2 + slot // OWN_COLS) * CELL_COLS + 2 + slot % OWN_COLS
        out[slot : slot + 1, :] = src[marks[cycle, cell] + at[0], pl.ds(marks[2 + cycle, cell] + at[1], 1), :]


def serial_slots(cycle, mid, got_even, got_odd, tables, acrosses, members, anomaly, change, beside=None):
    table = tables[cycle, :SLOTS, :]
    across = acrosses[cycle, :, :SLOTS]
    odd = parity("north") == 1
    south = jnp.where(odd, got_odd[...], got_even[...])
    north = jnp.where(odd, got_even[...], got_odd[...])
    flip = parity("east") == 0
    for third, source in enumerate((north, mid[...], south)):
        first, final = source[:OWN], source[2 * OWN :]
        west, east = jnp.where(flip, final, first), jnp.where(flip, first, final)
        for half in range(OWN_ROWS):
            base = (third * OWN_ROWS + half) * CELL_COLS
            own = half * OWN_COLS
            members[base : base + 2, :] = west[own + OWN_COLS - 2 : own + OWN_COLS]
            members[base + 2 : base + 2 + OWN_COLS, :] = source[OWN + own : OWN + own + OWN_COLS]
            members[base + 2 + OWN_COLS : base + CELL_COLS, :] = east[own : own + 2]
    lane = lax.broadcasted_iota(jnp.int32, (SLOTS, LANES), 1)
    prior = members[...]
    prior = jnp.where(lane < MEMBERS, prior, pltpu.roll(prior, MEMBERS, 1))
    value, noise, live = table[:, 0:1], table[:, 1:2], table[:, 2:3]
    near = jnp.maximum(0.0, 1.0 - jnp.abs(table[:, 3:4] - across[3:4, :]) / RADIUS)
    near = near * jnp.maximum(0.0, 1.0 - jnp.abs(table[:, 4:5] - across[4:5, :]) / RADIUS)
    turn_of = table[:, 5:6]
    kept_anomaly = jnp.zeros((SLOTS, LANES), F32)
    kept_change = jnp.zeros((SLOTS, LANES), F32)
    for batch in range(BATCHES):
        if beside is not None:
            beside(batch)
        now = turn_of == float(batch)
        mean = jnp.sum(prior, axis=1, keepdims=True) / LANES
        off = prior - mean
        spread = jnp.sum(off * off, axis=1, keepdims=True) / (2.0 * (MEMBERS - 1))
        gain = live / ((spread + noise) * (MEMBERS - 1))
        shrink = 1.0 / (1.0 + jnp.sqrt(noise / (spread + noise)))
        delta = jnp.where(now, gain * ((value - mean) - shrink * off), 0.0)
        kept_anomaly = jnp.where(now, off, kept_anomaly)
        kept_change = jnp.where(now, delta, kept_change)
        if batch < BATCHES - 1:
            cross = lax.dot_general(
                prior, off, (((1,), (1,)), ((), ())), precision=lax.Precision.HIGHEST, preferred_element_type=F32
            )
            prior = prior + jnp.dot(
                0.5 * near * cross, delta, precision=lax.Precision.HIGHEST, preferred_element_type=F32
            )
    anomaly[...] = kept_anomaly
    change[...] = kept_change


def windows(cycle, marks, state, anomaly, change, skirt):
    lane_in = lax.broadcasted_iota(jnp.int32, (2 * LANES, LANES), 0) % LANES
    lane_out = lax.broadcasted_iota(jnp.int32, (2 * LANES, LANES), 1)
    ones = ((lane_in // MEMBERS) == (lane_out // MEMBERS)).astype(BF16)
    offset = lax.broadcasted_iota(jnp.int32, (2 * RADIUS, LANES), 0) - (RADIUS - 1)
    lane = lax.broadcasted_iota(jnp.int32, (2 * RADIUS, LANES), 1)
    taper = jnp.maximum(0.0, 1.0 - jnp.abs(offset).astype(F32) / RADIUS)
    taper = taper * jnp.where(lane < MEMBERS, 1.0, LOWER_WEIGHT)
    count = CELL_COLS // 2 - 1
    shift = SIDE - (RADIUS - 1)
    reach = RADIUS - 1 + skirt

    def batch_step(batch, carry):
        colour = marks[4 + cycle, batch]
        down, right = colour // 2, colour % 2
        own = (2 + down) * CELL_COLS + 2 - right
        other = (4 - 3 * down) * CELL_COLS + 2 - right
        edge = (1 - down) * (ROWS + skirt - reach) - down * skirt
        held, products, weights, places = [], [], [], []

        def visit(cell, row, col, pattern, height):
            x = state[row + SIDE, pl.ds(col, 2 * RADIUS), :]
            held.append(x)
            products.append(x * pattern)
            weights.append(height)
            places.append((cell, row + SIDE, col))

        for i in range(count):
            cell = own + 2 * i
            row, col = marks[cycle, cell] - (RADIUS - 1), marks[2 + cycle, cell] + shift
            pattern = anomaly[pl.ds(cell, 1), :]
            for step in range(WINDOW):
                visit(cell, row + step, col, pattern, 1.0 - abs(step - (RADIUS - 1)) / RADIUS)
        for i in range(count):
            cell = other + 2 * i
            row, col = marks[cycle, cell], marks[2 + cycle, cell] + shift
            pattern = anomaly[pl.ds(cell, 1), :]
            for step in range(reach):
                height = jnp.maximum(0.0, 1.0 - jnp.abs(edge + step - row).astype(F32) / RADIUS)
                visit(cell, edge + step, col, pattern, height)
        product = jnp.concatenate(products, axis=0)
        high = product.astype(BF16)
        low = (product - high.astype(F32)).astype(BF16)
        moment = jnp.dot(jnp.concatenate([high, low], axis=1), ones, preferred_element_type=F32)
        for n, (cell, row, col) in enumerate(places):
            part = moment[n * 2 * RADIUS : (n + 1) * 2 * RADIUS] * (taper * weights[n])
            state[row, pl.ds(col, 2 * RADIUS), :] = held[n] + part * change[pl.ds(cell, 1), :]
        return carry

    lax.fori_loop(0, BATCHES, batch_step, 0)


GUIDES = [
    pltpu.VMEM((ANALYSES, LANES, LANES), F32),
    pltpu.VMEM((ANALYSES, 8, LANES), F32),
    MARKS,
    pltpu.VMEM((3 * OWN, LANES), F32),
    pltpu.VMEM((3 * OWN, LANES), F32),
    pltpu.VMEM((3 * OWN, LANES), F32),
]


def middle_kernel(*refs):
    guides_in, (ext_in, cast, result, slots), refs = refs[:6], refs[6:10], refs[10:]
    guides, refs = refs[:6], refs[6:]
    tables, acrosses, marks, mid, got_even, got_odd = guides
    ext_tiles, state, members, anomaly, change, one, two, out, coef, sems, late = refs
    copies = fetch([*zip(guides_in, guides), (ext_in, ext_tiles)], sems)
    big_copy = pltpu.make_async_copy(
        cast, state.at[pl.ds(SIDE - SKIRT, ROWS + 2 * SKIRT), pl.ds(SIDE - EDGE, EXT_COLS), :], late.at[0]
    )
    big_copy.start()
    matrix = spread_matrix()
    wait_for(copies)

    def beside(batch):
        spread_rows(ext_tiles, coef, matrix, -2, range(-2 + batch * 9, 7 + batch * 9))

    serial_slots(0, mid, got_even, got_odd, tables, acrosses, members, anomaly, change, beside)
    big_copy.wait()
    windows(0, marks, state, anomaly, change, SKIRT)
    big = (SIDE, SIDE)
    at = (2, 2 * EDGE)
    storage_step(state, big, None, big, one, at, coef, 2, -2, ROWS + 2, -1, EXT_COLS // 8)
    storage_step(one, at, state, big, two, at, coef, 2, -1, ROWS + 1, -1, EXT_COLS // 8)
    copies = []
    for part in range(4):
        cols = pl.ds(part * COLS // 4, COLS // 4)
        storage_step(two, at, state, big, out, (0, 0), coef, 2, 0, ROWS, 4 * part, 4)
        copy = pltpu.make_async_copy(out.at[:, cols, :], result.at[:, cols, :], late.at[part])
        copy.start()
        copies.append(copy)
    pick_slots(out, (0, 0), marks, 1, slots)
    wait_for(copies)


def middle(guides, gathered, ext_tiles, cast):
    return pl.pallas_call(
        middle_kernel,
        out_shape=(
            jax.ShapeDtypeStruct((ROWS, COLS, LANES), F32),
            jax.ShapeDtypeStruct((OWN, LANES), F32),
        ),
        in_specs=[HBM] * 8,
        out_specs=(HBM, VMEM),
        scratch_shapes=GUIDES
        + [pltpu.VMEM((4, EXT_COLS, LANES), F32), pltpu.VMEM((PAD_ROWS, PAD_COLS, LANES), F32)]
        + [pltpu.VMEM((SLOTS, LANES), F32)] * 3
        + [pltpu.VMEM((ROWS + 4, WIDE_COLS, LANES), F32)] * 2
        + [pltpu.VMEM((ROWS, COLS, LANES), F32), pltpu.VMEM((4, ROWS + 4, EXT_COLS, LANES), F32)]
        + [pltpu.SemaphoreType.DMA((7,)), pltpu.SemaphoreType.DMA((4,))],
        compiler_params=params(),
        name="middle",
    )(*guides, *gathered, ext_tiles, cast)


def last_kernel(*refs):
    guides_in, (cast, heads), refs = refs[:6], refs[6:8], refs[8:]
    guides, refs = refs[:6], refs[6:]
    tables, acrosses, marks, mid, got_even, got_odd = guides
    state, members, anomaly, change, out, sems, late = refs
    copies = fetch([*zip(guides_in, guides)], sems)
    big_copy = pltpu.make_async_copy(cast, state.at[pl.ds(SIDE, ROWS), pl.ds(SIDE, COLS), :], late.at[0])
    big_copy.start()
    wait_for(copies)
    serial_slots(1, mid, got_even, got_odd, tables, acrosses, members, anomaly, change)
    big_copy.wait()
    windows(1, marks, state, anomaly, change, 0)
    copies = []
    for part in range(ROWS // 8):
        for i in range(8):
            block = state[part * 8 + i + SIDE, SIDE : SIDE + COLS, :].T
            out.at[part].reshape(LANES * 8, COLS)[pl.ds(i, LANES, stride=8), :] = block
        copy = pltpu.make_async_copy(out.at[part], heads.at[:, pl.ds(part * 8, 8), :], late.at[part])
        copy.start()
        copies.append(copy)
    wait_for(copies)


def last(guides, gathered, cast):
    return pl.pallas_call(
        last_kernel,
        out_shape=jax.ShapeDtypeStruct((LANES, ROWS, COLS), F32),
        in_specs=[HBM] * 7,
        out_specs=HBM,
        scratch_shapes=GUIDES
        + [pltpu.VMEM((PAD_ROWS, PAD_COLS, LANES), F32)]
        + [pltpu.VMEM((SLOTS, LANES), F32)] * 3
        + [pltpu.VMEM((ROWS // 8, LANES, 8, COLS), F32)]
        + [pltpu.SemaphoreType.DMA((6,)), pltpu.SemaphoreType.DMA((4,))],
        compiler_params=params(),
        name="last",
    )(*guides, *gathered, cast)


def swap(x, axis, odd):
    peers = lax.axis_size(axis)
    low = range(odd, peers - 1, 2)
    return lax.ppermute(x, axis, [(i, i + 1) for i in low] + [(i + 1, i) for i in low])


def gather_slots(slots):
    even = swap(slots, "east", 0)
    odd = swap(slots, "east", 1)
    mid = jnp.concatenate([even, slots, odd], axis=0)
    return mid, swap(mid, "north", 0), swap(mid, "north", 1)


def table_kernel(colours, value, noise, spot, live, after, tables, acrosses, marks, stacked):
    tall, wide = value.shape[2:]
    lat_row = lax.axis_index("north") - 1
    lat_col = lax.axis_index("east") * (COLS // (2 * SPAN)) - 1
    top = lax.Precision.HIGHEST
    spread = 2 * CELL_ROWS
    out_row = lax.broadcasted_iota(jnp.int32, (spread, tall), 0)
    in_row = lax.broadcasted_iota(jnp.int32, (spread, tall), 1)
    in_col = lax.broadcasted_iota(jnp.int32, (wide, LANES), 0)
    cell = lax.broadcasted_iota(jnp.int32, (wide, LANES), 1)
    take_col = (in_col == lat_col + cell % CELL_COLS // 2).astype(F32)
    got_row = lax.broadcasted_iota(jnp.int32, (spread, LANES), 0)
    lane = lax.broadcasted_iota(jnp.int32, (spread, LANES), 1)
    kept = (got_row // 2 == lane // CELL_COLS) & (got_row % 2 == lane % CELL_COLS % 2) & (lane < SLOTS)
    index = lax.broadcasted_iota(jnp.int32, (1, LANES), 1)
    cell_row, cell_col = index // CELL_COLS, index % CELL_COLS
    marks[...] = jnp.zeros_like(marks)
    for cycle in range(ANALYSES):
        turn = jnp.zeros((1, LANES), F32)
        rows_of = []
        for batch in range(BATCHES):
            colour = colours[cycle, batch]
            down, right = colour // 2, colour % 2
            wanted = (in_row == lat_row + out_row // 4) & (out_row // 2 % 2 == down) & (out_row % 2 == right)
            rows_of.append(wanted.astype(F32))
            mine = (cell_row % 2 == down) & (cell_col % 2 == right)
            turn = jnp.where(mine, float(batch), turn)
        picker = jnp.concatenate(rows_of, axis=1)
        fields = []
        for source in (value, noise, spot, live):
            whole = jnp.concatenate([source[cycle, batch].astype(F32) for batch in range(BATCHES)], axis=0)
            part = jnp.dot(picker, whole, precision=top, preferred_element_type=F32)
            part = jnp.dot(part, take_col, precision=top, preferred_element_type=F32)
            fields.append(jnp.sum(jnp.where(kept, part, 0.0), axis=0, keepdims=True))
        of_value, of_noise, of_spot, of_live = fields
        of_noise = jnp.where(of_noise > 0.0, of_noise, 1.0)
        place = (of_spot + 0.5).astype(jnp.int32)
        row = (cell_row - 2) * SPAN + place // SPAN
        col = (cell_col - 2) * SPAN + place % SPAN
        marks[cycle : cycle + 1, :] = row
        marks[2 + cycle : 3 + cycle, :] = col
        chosen = jnp.zeros((1, LANES), jnp.int32)
        for batch in range(BATCHES):
            chosen = jnp.where(index == batch, colours[cycle, batch], chosen)
        marks[4 + cycle : 5 + cycle, :] = chosen
        block = jnp.concatenate(
            [of_value, of_noise, of_live, row.astype(F32), col.astype(F32), turn, turn, turn], axis=0
        )
        acrosses[cycle] = block
        stacked[...] = jnp.zeros_like(stacked)
        stacked[:8, :] = block
        tables[cycle] = stacked[...].T


def slot_tables(obs_value, obs_error, obs_spot, obs_live, batch_colour, after):
    return pl.pallas_call(
        table_kernel,
        out_shape=(
            jax.ShapeDtypeStruct((ANALYSES, LANES, LANES), F32),
            jax.ShapeDtypeStruct((ANALYSES, 8, LANES), F32),
            jax.ShapeDtypeStruct((8, LANES), jnp.int32),
        ),
        in_specs=[SMEM] + [VMEM] * 4 + [HBM],
        out_specs=(VMEM, VMEM, VMEM),
        scratch_shapes=[pltpu.VMEM((LANES, LANES), F32)],
        compiler_params=params(),
        cost_estimate=weight(3),
        name="slot_tables",
    )(batch_colour, obs_value, obs_error, obs_spot, obs_live, after)


def shards(
    head_ensemble,
    transmissivity_grid,
    interlayer_leakage_factor,
    specific_porosity_release,
    infiltration_inflow,
    obs_value,
    obs_error,
    obs_spot,
    obs_live,
    batch_colour,
):
    heads = head_ensemble.reshape(LANES, ROWS, COLS)
    tiles, give_even, give_odd = edges(
        heads, transmissivity_grid, interlayer_leakage_factor, specific_porosity_release, infiltration_inflow
    )
    ns_even, ns_odd = swap(give_even, "north", 0), swap(give_odd, "north", 1)
    turned, give_even, give_odd = turn(heads.reshape(LANES * ROWS, COLS), tiles)
    ew_even, ew_odd = swap(give_even, "east", 0), swap(give_odd, "east", 1)
    give_even, give_odd = corners(ns_even, ns_odd)
    corner_even, corner_odd = swap(give_even, "east", 0), swap(give_odd, "east", 1)
    guides = slot_tables(obs_value, obs_error, obs_spot, obs_live, batch_colour, give_even)
    pieces = (turned, tiles, ns_even, ns_odd, ew_even, ew_odd, corner_even, corner_odd)
    cast, slots, ext_tiles = first_forecast(pieces, guides[2])
    gathered = gather_slots(slots)
    cast, slots = middle(guides, gathered, ext_tiles, cast)
    gathered = gather_slots(slots)
    out = last(guides, gathered, cast)
    return out.reshape(2, MEMBERS, ROWS, COLS)


def solution(mesh):
    placed = (
        P(None, None, "north", "east"),
        P(None, "north", "east"),
        P("north", "east"),
        P("north", "east"),
        P("north", "east"),
        P(),
        P(),
        P(),
        P(),
        P(),
    )
    return jax.shard_map(
        shards,
        mesh=mesh,
        in_specs=placed,
        out_specs=P(None, None, "north", "east"),
        check_vma=False,
    )
```

```python
import jax
import jax.numpy as jnp
from jax import lax
from jax.experimental import pallas as pl
from jax.experimental.pallas import tpu as pltpu
from jax.sharding import PartitionSpec as P

ITERS = 3
ANALYSES = 2
BATCHES = 4
MEMBERS = 64
RADIUS = 8
SPAN = 16
LOWER_WEIGHT = 0.6
LANES = 128

ROWS = 32
COLS = 128
HALO = 6
EDGE = 8
SKIRT = 3
EXT_ROWS = ROWS + 2 * HALO
EXT_COLS = COLS + 2 * EDGE
WIDE_COLS = EXT_COLS + 2 * EDGE
SIDE = 24
PAD_ROWS = 80
PAD_COLS = 184
CELL_ROWS = 6
CELL_COLS = 12
SLOTS = CELL_ROWS * CELL_COLS
OWN_ROWS = 2
OWN_COLS = 8
OWN = OWN_ROWS * OWN_COLS
GROUP_COLS = 48
KINDS = 8
WINDOW = 2 * RADIUS - 1

VMEM_BYTES = 64 * 2**20

F32 = jnp.float32
BF16 = jnp.bfloat16
SMEM = pl.BlockSpec(memory_space=pltpu.SMEM)
VMEM = pl.BlockSpec(memory_space=pltpu.VMEM)
HBM = pl.BlockSpec(memory_space=pltpu.HBM)
MARKS = pltpu.SMEM((8, LANES), jnp.int32)


def params():
    return pltpu.CompilerParams(vmem_limit_bytes=VMEM_BYTES)


def weight(microseconds):
    return pl.CostEstimate(flops=0, bytes_accessed=int(microseconds * 3.5e6), transcendentals=0)


def parity(axis):
    return lax.axis_index(axis) % 2


def edge_kernel(top, bottom, transmissivity, leakage, release, inflow, tiles, give_even, give_odd, stacked):
    stacked[...] = jnp.zeros_like(stacked)
    for half in range(2):
        part = slice(half * SPAN, (half + 1) * SPAN)
        for kind, field in enumerate((transmissivity.at[0], transmissivity.at[1], leakage, release, inflow)):
            stacked[pl.ds(half * LANES + kind, SPAN, stride=KINDS), :] = field[part, :]
        tiles[half] = stacked[half * LANES : (half + 1) * LANES, :].T
    odd = parity("north")
    for row in range(HALO):
        upper = top[pl.ds(row, LANES, stride=8), :].T
        lower = bottom[pl.ds(8 - HALO + row, LANES, stride=8), :].T
        give_even[row] = jnp.where(odd == 0, lower, upper)
        give_odd[row] = jnp.where(odd == 0, upper, lower)
    give_even[HALO] = tiles[1 - odd]
    give_odd[HALO] = tiles[odd]


def edges(heads, transmissivity, leakage, release, inflow):
    def rows_at(at):
        return pl.BlockSpec((LANES, 8, COLS), lambda i: (0, at, 0))

    def kernel(top, bottom, *rest):
        edge_kernel(top.reshape(LANES * 8, COLS), bottom.reshape(LANES * 8, COLS), *rest)

    halo = jax.ShapeDtypeStruct((HALO + 1, COLS, LANES), F32)
    return pl.pallas_call(
        kernel,
        grid=(1,),
        out_shape=(jax.ShapeDtypeStruct((2, COLS, LANES), F32), halo, halo),
        in_specs=[rows_at(0), rows_at(ROWS // 8 - 1)] + [VMEM] * 4,
        out_specs=(VMEM, VMEM, VMEM),
        scratch_shapes=[pltpu.VMEM((2 * LANES, COLS), F32)],
        compiler_params=params(),
        name="edges",
    )(heads, heads, transmissivity, leakage, release, inflow)


def turn_kernel(heads, tiles, turned, give_even, give_odd):
    def body(row, carry):
        turned[row] = heads[pl.ds(row, LANES, stride=ROWS), :].T
        return carry

    lax.fori_loop(0, ROWS, body, 0, unroll=16)
    odd = parity("east")
    for give, at in ((give_even, 1 - odd), (give_odd, odd)):
        cols = pl.ds(pl.multiple_of(at * (COLS - EDGE), EDGE), EDGE)
        give[:ROWS] = turned[:, cols, :]
        give[ROWS:] = tiles[:, cols, :]


def turn(heads, tiles):
    strip = jax.ShapeDtypeStruct((ROWS + 2, EDGE, LANES), F32)
    return pl.pallas_call(
        turn_kernel,
        out_shape=(jax.ShapeDtypeStruct((ROWS, COLS, LANES), F32), strip, strip),
        in_specs=[VMEM, VMEM],
        out_specs=(VMEM, VMEM, VMEM),
        compiler_params=params(),
        cost_estimate=weight(4),
        name="turn",
    )(heads, tiles)


def corner_kernel(even_left, even_right, odd_left, odd_right, give_even, give_odd):
    flip_n = parity("north") == 0
    flip_e = parity("east") == 0
    for half, swap_n in enumerate((flip_n, jnp.logical_not(flip_n))):
        left = jnp.where(swap_n, odd_left[...], even_left[...])
        right = jnp.where(swap_n, odd_right[...], even_right[...])
        part = slice(half * (HALO + 1), (half + 1) * (HALO + 1))
        give_even[part] = jnp.where(flip_e, right, left)
        give_odd[part] = jnp.where(flip_e, left, right)


def corners(got_even, got_odd):
    def cut(at):
        return pl.BlockSpec((HALO + 1, EDGE, LANES), lambda i: (0, at, 0))

    last = COLS // EDGE - 1
    whole = pl.BlockSpec((2 * HALO + 2, EDGE, LANES), lambda i: (0, 0, 0))
    shape = jax.ShapeDtypeStruct((2 * HALO + 2, EDGE, LANES), F32)
    return pl.pallas_call(
        corner_kernel,
        grid=(1,),
        out_shape=(shape, shape),
        in_specs=[cut(0), cut(last), cut(0), cut(last)],
        out_specs=(whole, whole),
        compiler_params=params(),
        name="corners",
    )(got_even, got_even, got_odd, got_odd)


def spread_matrix():
    lane = lax.broadcasted_iota(jnp.int32, (2 * LANES, 4 * LANES), 0) % KINDS
    out = lax.broadcasted_iota(jnp.int32, (2 * LANES, 4 * LANES), 1)
    group = out // LANES
    lower = out % LANES >= MEMBERS
    wanted = jnp.where(group == 0, jnp.where(lower, 1, 0), group + 1)
    wanted = jnp.where((group == 3) & lower, KINDS, wanted)
    return (lane == wanted).astype(BF16)


def spread_rows(tiles, coef, matrix, first, rows):
    owner = lax.broadcasted_iota(jnp.int32, (EXT_COLS, LANES), 1) // KINDS
    parts = []
    for row in rows:
        parts.append(jnp.where(owner == (row + SPAN) % SPAN, tiles[(row + SPAN) // SPAN], 0.0))
    tile = jnp.concatenate(parts, axis=0)
    high = tile.astype(BF16)
    low = (tile - high.astype(F32)).astype(BF16)
    wide = jnp.dot(jnp.concatenate([high, low], axis=1), matrix, preferred_element_type=F32)
    for i, row in enumerate(rows):
        for kind in range(4):
            coef[kind, row - first] = wide[i * EXT_COLS : (i + 1) * EXT_COLS, kind * LANES : (kind + 1) * LANES]


def storage(u, around, start, factors):
    lateral, leakage, release, inflow = factors
    exchange = pltpu.roll(u, MEMBERS, 1) - u
    top = lateral * (around - 4.0 * u) + leakage * exchange + inflow
    bottom = release * (1.0 + jnp.tanh(0.5 * u)) + 1.0
    return start + top * pltpu.reciprocal(bottom, approx=True)


def storage_step(src, src_at, start, start_at, dst, dst_at, coef, coef_at, low, high, first, count, unroll=None):
    def strip(tile, carry):
        col = tile * 8 if unroll is None else pl.multiple_of(tile * 8, 8)

        def read(ref, at, row, shift=0):
            return ref[row + at[0], pl.ds(at[1] + 8 * first + shift + col, 8), :]

        above, u = read(src, src_at, low - 1), read(src, src_at, low)
        for row in range(low, high):
            below = read(src, src_at, row + 1)
            around = (above + below) + (read(src, src_at, row, -1) + read(src, src_at, row, 1))
            held = u if start is None else read(start, start_at, row)
            factors = [coef[kind, row + coef_at, pl.ds(EDGE + 8 * first + col, 8), :] for kind in range(4)]
            dst[row + dst_at[0], pl.ds(dst_at[1] + 8 * first + col, 8), :] = storage(u, around, held, factors)
            above, u = u, below
        return carry

    if unroll is None:
        for tile in range(count):
            strip(tile, 0)
    else:
        lax.fori_loop(0, count, strip, 0, unroll=unroll)


def fetch(pairs, sems):
    copies = [pltpu.make_async_copy(a, b, sems.at[i]) for i, (a, b) in enumerate(pairs)]
    for copy in copies:
        copy.start()
    return copies


def wait_for(copies):
    for copy in copies:
        copy.wait()


def first_kernel(
    turned, tiles, ns_even, ns_odd, ew_even, ew_odd, corner_even, corner_odd, marks_in,
    cast, slots, ext_tiles, start, one, two, coef, marks, tile_sems, sems,
):
    odd_n, odd_e = parity("north"), parity("east")
    even_row = (1 - odd_n) * (ROWS + HALO)
    odd_row = odd_n * (ROWS + HALO)
    even_col = (1 - odd_e) * (COLS + EDGE)
    odd_col = odd_e * (COLS + EDGE)
    inner = pl.ds(2 * EDGE, COLS)
    tile_inner = pl.ds(EDGE, COLS)
    moves = [
        (turned, start.at[pl.ds(HALO, ROWS), inner, :]),
        (ns_even.at[pl.ds(0, HALO)], start.at[pl.ds(even_row, HALO), inner, :]),
        (ns_odd.at[pl.ds(0, HALO)], start.at[pl.ds(odd_row, HALO), inner, :]),
    ]
    tile_moves = [
        (tiles, ext_tiles.at[pl.ds(1, 2), tile_inner, :]),
        (ns_even.at[pl.ds(HALO, 1)], ext_tiles.at[pl.ds((1 - odd_n) * 3, 1), tile_inner, :]),
        (ns_odd.at[pl.ds(HALO, 1)], ext_tiles.at[pl.ds(odd_n * 3, 1), tile_inner, :]),
    ]
    for at, strip, corner in ((even_col, ew_even, corner_even), (odd_col, ew_odd, corner_odd)):
        outer = pl.ds(pl.multiple_of(at + EDGE, EDGE), EDGE)
        tile_outer = pl.ds(pl.multiple_of(at, EDGE), EDGE)
        moves += [
            (strip.at[pl.ds(0, ROWS)], start.at[pl.ds(HALO, ROWS), outer, :]),
            (corner.at[pl.ds(0, HALO)], start.at[pl.ds(0, HALO), outer, :]),
            (corner.at[pl.ds(HALO + 1, HALO)], start.at[pl.ds(HALO + ROWS, HALO), outer, :]),
        ]
        tile_moves += [
            (strip.at[pl.ds(ROWS, 2)], ext_tiles.at[pl.ds(1, 2), tile_outer, :]),
            (corner.at[pl.ds(HALO, 1)], ext_tiles.at[pl.ds(0, 1), tile_outer, :]),
            (corner.at[pl.ds(2 * HALO + 1, 1)], ext_tiles.at[pl.ds(3, 1), tile_outer, :]),
        ]
    tile_copies = fetch(tile_moves, tile_sems)
    copies = fetch(moves + [(marks_in, marks)], sems)
    matrix = spread_matrix()
    wait_for(tile_copies)
    wait_for(copies)
    at = (HALO, 2 * EDGE)
    count = EXT_COLS // 8
    owner = lax.broadcasted_iota(jnp.int32, (GROUP_COLS, LANES), 1) // KINDS

    def body(group, carry):
        col = pl.multiple_of(group * GROUP_COLS, GROUP_COLS)
        needed = range(1 - HALO, ROWS + HALO - 1)
        parts = []
        for row in needed:
            tile = ext_tiles[(row + SPAN) // SPAN, pl.ds(col, GROUP_COLS), :]
            parts.append(jnp.where(owner == (row + SPAN) % SPAN, tile, 0.0))
        tile = jnp.concatenate(parts, axis=0)
        high = tile.astype(BF16)
        low = (tile - high.astype(F32)).astype(BF16)
        wide = jnp.dot(jnp.concatenate([high, low], axis=1), matrix, preferred_element_type=F32)
        for piece in range(GROUP_COLS // 8):
            aside = EDGE + 8 * piece
            above = start[0, pl.ds(col + aside, 8), :]
            u = start[1, pl.ds(col + aside, 8), :]
            for i, row in enumerate(needed):
                at_row = row + HALO
                below = start[at_row + 1, pl.ds(col + aside, 8), :]
                left = start[at_row, pl.ds(col + aside - 1, 8), :]
                right = start[at_row, pl.ds(col + aside + 1, 8), :]
                block = i * GROUP_COLS + 8 * piece
                factors = [wide[block : block + 8, kind * LANES : (kind + 1) * LANES] for kind in range(4)]
                for kind in range(4):
                    coef[kind, at_row, pl.ds(col + 8 * piece, 8), :] = factors[kind]
                one[at_row, pl.ds(col + aside, 8), :] = storage(u, (above + below) + (left + right), u, factors)
                above, u = u, below
        return carry

    lax.fori_loop(0, EXT_COLS // GROUP_COLS, body, 0)
    storage_step(one, at, start, at, two, at, coef, HALO, -4, ROWS + 4, -1, count, 9)
    copies = []
    for part in range(3):
        first = -1 + part * count // 3
        storage_step(two, at, start, at, one, at, coef, HALO, -SKIRT, ROWS + SKIRT, first, count // 3, 6)
        copy = pltpu.make_async_copy(
            one.at[pl.ds(HALO - SKIRT, ROWS + 2 * SKIRT), pl.ds(2 * EDGE + 8 * first, 8 * count // 3), :],
            cast.at[:, pl.ds(EDGE + 8 * first, 8 * count // 3), :],
            sems.at[part],
        )
        copy.start()
        copies.append(copy)
    pick_slots(one, at, marks, 0, slots)
    wait_for(copies)


def first_forecast(pieces, marks):
    return pl.pallas_call(
        first_kernel,
        out_shape=(
            jax.ShapeDtypeStruct((ROWS + 2 * SKIRT, EXT_COLS, LANES), F32),
            jax.ShapeDtypeStruct((OWN, LANES), F32),
            jax.ShapeDtypeStruct((4, EXT_COLS, LANES), F32),
        ),
        in_specs=[HBM] * 9,
        out_specs=(HBM, VMEM, VMEM),
        scratch_shapes=[pltpu.VMEM((EXT_ROWS, WIDE_COLS, LANES), F32)] * 3
        + [pltpu.VMEM((4, EXT_ROWS, EXT_COLS, LANES), F32)]
        + [MARKS, pltpu.SemaphoreType.DMA((9,)), pltpu.SemaphoreType.DMA((10,))],
        compiler_params=params(),
        name="first_forecast",
    )(*pieces, marks)


def pick_slots(src, at, marks, cycle, out):
    for slot in range(OWN):
        cell = (2 + slot // OWN_COLS) * CELL_COLS + 2 + slot % OWN_COLS
        out[slot : slot + 1, :] = src[marks[cycle, cell] + at[0], pl.ds(marks[2 + cycle, cell] + at[1], 1), :]


def halves(x):
    high = x.astype(BF16)
    return high, (x - high.astype(F32)).astype(BF16)


def serial_slots(cycle, mid, got_even, got_odd, tables, acrosses, members, anomaly, change, beside=None):
    table = tables[cycle, :SLOTS, :]
    across = acrosses[cycle]
    odd = parity("north") == 1
    south = jnp.where(odd, got_odd[...], got_even[...])
    north = jnp.where(odd, got_even[...], got_odd[...])
    flip = parity("east") == 0
    for third, source in enumerate((north, mid[...], south)):
        first, final = source[:OWN], source[2 * OWN :]
        west, east = jnp.where(flip, first, final), jnp.where(flip, final, first)
        for half in range(OWN_ROWS):
            base = (third * OWN_ROWS + half) * CELL_COLS
            own = half * OWN_COLS
            members[base : base + 2, :] = west[own + OWN_COLS - 2 : own + OWN_COLS]
            members[base + 2 : base + 2 + OWN_COLS, :] = source[OWN + own : OWN + own + OWN_COLS]
            members[base + 2 + OWN_COLS : base + CELL_COLS, :] = east[own : own + 2]
    lane = lax.broadcasted_iota(jnp.int32, (SLOTS, LANES), 1)
    prior = members[...]
    prior = jnp.where(lane < MEMBERS, prior, pltpu.roll(prior, MEMBERS, 1))
    value, noise, live = table[:, 0:1], table[:, 1:2], table[:, 2:3]
    near = jnp.maximum(0.0, 1.0 - jnp.abs(table[:, 3:4] - across[3:4, :]) / RADIUS)
    near = near * jnp.maximum(0.0, 1.0 - jnp.abs(table[:, 4:5] - across[4:5, :]) / RADIUS)
    turn_of = table[:, 5:6]
    spare = jnp.zeros((LANES - SLOTS, LANES), F32)
    kept_anomaly = jnp.zeros((SLOTS, LANES), F32)
    kept_change = jnp.zeros((SLOTS, LANES), F32)
    for batch in range(BATCHES):
        if beside is not None:
            beside(batch)
        now = turn_of == float(batch)
        mean = jnp.sum(prior, axis=1, keepdims=True) / LANES
        off = prior - mean
        spread = jnp.sum(off * off, axis=1, keepdims=True) / (2.0 * (MEMBERS - 1))
        gain = live / ((spread + noise) * (MEMBERS - 1))
        shrink = 1.0 / (1.0 + jnp.sqrt(noise / (spread + noise)))
        delta = jnp.where(now, gain * ((value - mean) - shrink * off), 0.0)
        kept_anomaly = jnp.where(now, off, kept_anomaly)
        kept_change = jnp.where(now, delta, kept_change)
        if batch < BATCHES - 1:
            high, low = halves(prior)
            off_high, off_low = halves(jnp.concatenate([off, spare], axis=0))
            cross = lax.dot_general(
                jnp.concatenate([high, high, low], axis=1),
                jnp.concatenate([off_high, off_low, off_high], axis=1),
                (((1,), (1,)), ((), ())),
                preferred_element_type=F32,
            )
            high, low = halves(0.5 * near * cross)
            delta_high, delta_low = halves(jnp.concatenate([delta, spare], axis=0))
            prior = prior + jnp.dot(
                jnp.concatenate([high, high, low], axis=1),
                jnp.concatenate([delta_high, delta_low, delta_high], axis=0),
                preferred_element_type=F32,
            )
    anomaly[...] = kept_anomaly
    change[...] = kept_change


def windows(cycle, marks, state, anomaly, change, skirt):
    lane_in = lax.broadcasted_iota(jnp.int32, (2 * LANES, LANES), 0) % LANES
    lane_out = lax.broadcasted_iota(jnp.int32, (2 * LANES, LANES), 1)
    ones = ((lane_in // MEMBERS) == (lane_out // MEMBERS)).astype(BF16)
    offset = lax.broadcasted_iota(jnp.int32, (2 * RADIUS, LANES), 0) - (RADIUS - 1)
    lane = lax.broadcasted_iota(jnp.int32, (2 * RADIUS, LANES), 1)
    taper = jnp.maximum(0.0, 1.0 - jnp.abs(offset).astype(F32) / RADIUS)
    taper = taper * jnp.where(lane < MEMBERS, 1.0, LOWER_WEIGHT)
    count = CELL_COLS // 2 - 1
    shift = SIDE - (RADIUS - 1)
    reach = RADIUS - 1 + skirt

    def batch_step(batch, carry):
        colour = marks[4 + cycle, batch]
        down, right = colour // 2, colour % 2
        own = (2 + down) * CELL_COLS + 2 - right
        other = (4 - 3 * down) * CELL_COLS + 2 - right
        edge = (1 - down) * (ROWS + skirt - reach) - down * skirt
        held, products, weights, places = [], [], [], []

        def visit(cell, row, col, pattern, height):
            x = state[row + SIDE, pl.ds(col, 2 * RADIUS), :]
            held.append(x)
            products.append(x * pattern)
            weights.append(height)
            places.append((cell, row + SIDE, col))

        for i in range(count):
            cell = own + 2 * i
            row, col = marks[cycle, cell] - (RADIUS - 1), marks[2 + cycle, cell] + shift
            pattern = anomaly[pl.ds(cell, 1), :]
            for step in range(WINDOW):
                visit(cell, row + step, col, pattern, 1.0 - abs(step - (RADIUS - 1)) / RADIUS)
        for i in range(count):
            cell = other + 2 * i
            row, col = marks[cycle, cell], marks[2 + cycle, cell] + shift
            pattern = anomaly[pl.ds(cell, 1), :]
            for step in range(reach):
                height = jnp.maximum(0.0, 1.0 - jnp.abs(edge + step - row).astype(F32) / RADIUS)
                visit(cell, edge + step, col, pattern, height)
        product = jnp.concatenate(products, axis=0)
        high = product.astype(BF16)
        low = (product - high.astype(F32)).astype(BF16)
        moment = jnp.dot(jnp.concatenate([high, low], axis=1), ones, preferred_element_type=F32)
        for n, (cell, row, col) in enumerate(places):
            part = moment[n * 2 * RADIUS : (n + 1) * 2 * RADIUS] * (taper * weights[n])
            state[row, pl.ds(col, 2 * RADIUS), :] = held[n] + part * change[pl.ds(cell, 1), :]
        return carry

    lax.fori_loop(0, BATCHES, batch_step, 0)


GUIDES = [
    pltpu.VMEM((ANALYSES, LANES, LANES), F32),
    pltpu.VMEM((ANALYSES, 8, LANES), F32),
    MARKS,
    pltpu.VMEM((3 * OWN, LANES), F32),
    pltpu.VMEM((3 * OWN, LANES), F32),
    pltpu.VMEM((3 * OWN, LANES), F32),
]


def middle_kernel(*refs):
    guides_in, (ext_in, cast, result, slots), refs = refs[:6], refs[6:10], refs[10:]
    guides, refs = refs[:6], refs[6:]
    tables, acrosses, marks, mid, got_even, got_odd = guides
    ext_tiles, state, members, anomaly, change, one, two, out, coef, sems, late = refs
    copies = fetch([*zip(guides_in, guides), (ext_in, ext_tiles)], sems)
    big_copy = pltpu.make_async_copy(
        cast, state.at[pl.ds(SIDE - SKIRT, ROWS + 2 * SKIRT), pl.ds(SIDE - EDGE, EXT_COLS), :], late.at[0]
    )
    big_copy.start()
    matrix = spread_matrix()
    wait_for(copies)

    def beside(batch):
        spread_rows(ext_tiles, coef, matrix, -2, range(-2 + batch * 9, 7 + batch * 9))

    serial_slots(0, mid, got_even, got_odd, tables, acrosses, members, anomaly, change, beside)
    big_copy.wait()
    windows(0, marks, state, anomaly, change, SKIRT)
    big = (SIDE, SIDE)
    at = (2, 2 * EDGE)
    storage_step(state, big, None, big, one, at, coef, 2, -2, ROWS + 2, -1, EXT_COLS // 8)
    storage_step(one, at, state, big, two, at, coef, 2, -1, ROWS + 1, -1, EXT_COLS // 8)
    copies = []
    for part in range(4):
        cols = pl.ds(part * COLS // 4, COLS // 4)
        storage_step(two, at, state, big, out, (0, 0), coef, 2, 0, ROWS, 4 * part, 4)
        copy = pltpu.make_async_copy(out.at[:, cols, :], result.at[:, cols, :], late.at[part])
        copy.start()
        copies.append(copy)
    pick_slots(out, (0, 0), marks, 1, slots)
    wait_for(copies)


def middle(guides, gathered, ext_tiles, cast):
    return pl.pallas_call(
        middle_kernel,
        out_shape=(
            jax.ShapeDtypeStruct((ROWS, COLS, LANES), F32),
            jax.ShapeDtypeStruct((OWN, LANES), F32),
        ),
        in_specs=[HBM] * 8,
        out_specs=(HBM, VMEM),
        scratch_shapes=GUIDES
        + [pltpu.VMEM((4, EXT_COLS, LANES), F32), pltpu.VMEM((PAD_ROWS, PAD_COLS, LANES), F32)]
        + [pltpu.VMEM((SLOTS, LANES), F32)] * 3
        + [pltpu.VMEM((ROWS + 4, WIDE_COLS, LANES), F32)] * 2
        + [pltpu.VMEM((ROWS, COLS, LANES), F32), pltpu.VMEM((4, ROWS + 4, EXT_COLS, LANES), F32)]
        + [pltpu.SemaphoreType.DMA((7,)), pltpu.SemaphoreType.DMA((4,))],
        compiler_params=params(),
        name="middle",
    )(*guides, *gathered, ext_tiles, cast)


def last_kernel(*refs):
    guides_in, (cast, heads), refs = refs[:6], refs[6:8], refs[8:]
    guides, refs = refs[:6], refs[6:]
    tables, acrosses, marks, mid, got_even, got_odd = guides
    state, members, anomaly, change, out, sems, late = refs
    copies = fetch([*zip(guides_in, guides)], sems)
    big_copy = pltpu.make_async_copy(cast, state.at[pl.ds(SIDE, ROWS), pl.ds(SIDE, COLS), :], late.at[0])
    big_copy.start()
    wait_for(copies)
    serial_slots(1, mid, got_even, got_odd, tables, acrosses, members, anomaly, change)
    big_copy.wait()
    windows(1, marks, state, anomaly, change, 0)
    copies = []
    for part in range(ROWS // 8):
        for i in range(8):
            block = state[part * 8 + i + SIDE, SIDE : SIDE + COLS, :].T
            out.at[part].reshape(LANES * 8, COLS)[pl.ds(i, LANES, stride=8), :] = block
        copy = pltpu.make_async_copy(out.at[part], heads.at[:, pl.ds(part * 8, 8), :], late.at[part])
        copy.start()
        copies.append(copy)
    wait_for(copies)


def last(guides, gathered, cast):
    return pl.pallas_call(
        last_kernel,
        out_shape=jax.ShapeDtypeStruct((LANES, ROWS, COLS), F32),
        in_specs=[HBM] * 7,
        out_specs=HBM,
        scratch_shapes=GUIDES
        + [pltpu.VMEM((PAD_ROWS, PAD_COLS, LANES), F32)]
        + [pltpu.VMEM((SLOTS, LANES), F32)] * 3
        + [pltpu.VMEM((ROWS // 8, LANES, 8, COLS), F32)]
        + [pltpu.SemaphoreType.DMA((6,)), pltpu.SemaphoreType.DMA((4,))],
        compiler_params=params(),
        name="last",
    )(*guides, *gathered, cast)


def swap(x, axis, odd):
    peers = lax.axis_size(axis)
    low = range(odd, peers - 1, 2)
    return lax.ppermute(x, axis, [(i, i + 1) for i in low] + [(i + 1, i) for i in low])


def gather_slots(slots):
    odd = swap(slots, "east", 1)
    even = swap(slots, "east", 0)
    mid = jnp.concatenate([odd, slots, even], axis=0)
    return mid, swap(mid, "north", 0), swap(mid, "north", 1)


def table_kernel(colours, value, noise, spot, live, after, tables, acrosses, marks, stacked):
    tall, wide = value.shape[2:]
    lat_row = lax.axis_index("north") - 1
    lat_col = lax.axis_index("east") * (COLS // (2 * SPAN)) - 1
    top = lax.Precision.HIGHEST
    spread = 2 * CELL_ROWS
    out_row = lax.broadcasted_iota(jnp.int32, (spread, tall), 0)
    in_row = lax.broadcasted_iota(jnp.int32, (spread, tall), 1)
    in_col = lax.broadcasted_iota(jnp.int32, (wide, LANES), 0)
    cell = lax.broadcasted_iota(jnp.int32, (wide, LANES), 1)
    take_col = (in_col == lat_col + cell % CELL_COLS // 2).astype(F32)
    got_row = lax.broadcasted_iota(jnp.int32, (spread, LANES), 0)
    lane = lax.broadcasted_iota(jnp.int32, (spread, LANES), 1)
    kept = (got_row // 2 == lane // CELL_COLS) & (got_row % 2 == lane % CELL_COLS % 2) & (lane < SLOTS)
    index = lax.broadcasted_iota(jnp.int32, (1, LANES), 1)
    cell_row, cell_col = index // CELL_COLS, index % CELL_COLS
    marks[...] = jnp.zeros_like(marks)
    for cycle in range(ANALYSES):
        turn = jnp.zeros((1, LANES), F32)
        rows_of = []
        for batch in range(BATCHES):
            colour = colours[cycle, batch]
            down, right = colour // 2, colour % 2
            wanted = (in_row == lat_row + out_row // 4) & (out_row // 2 % 2 == down) & (out_row % 2 == right)
            rows_of.append(wanted.astype(F32))
            mine = (cell_row % 2 == down) & (cell_col % 2 == right)
            turn = jnp.where(mine, float(batch), turn)
        picker = jnp.concatenate(rows_of, axis=1)
        fields = []
        for source in (value, noise, spot, live):
            whole = jnp.concatenate([source[cycle, batch].astype(F32) for batch in range(BATCHES)], axis=0)
            part = jnp.dot(picker, whole, precision=top, preferred_element_type=F32)
            part = jnp.dot(part, take_col, precision=top, preferred_element_type=F32)
            fields.append(jnp.sum(jnp.where(kept, part, 0.0), axis=0, keepdims=True))
        of_value, of_noise, of_spot, of_live = fields
        of_noise = jnp.where(of_noise > 0.0, of_noise, 1.0)
        place = (of_spot + 0.5).astype(jnp.int32)
        row = (cell_row - 2) * SPAN + place // SPAN
        col = (cell_col - 2) * SPAN + place % SPAN
        marks[cycle : cycle + 1, :] = row
        marks[2 + cycle : 3 + cycle, :] = col
        chosen = jnp.zeros((1, LANES), jnp.int32)
        for batch in range(BATCHES):
            chosen = jnp.where(index == batch, colours[cycle, batch], chosen)
        marks[4 + cycle : 5 + cycle, :] = chosen
        block = jnp.concatenate(
            [of_value, of_noise, of_live, row.astype(F32), col.astype(F32), turn, turn, turn], axis=0
        )
        acrosses[cycle] = block
        stacked[...] = jnp.zeros_like(stacked)
        stacked[:8, :] = block
        tables[cycle] = stacked[...].T


def slot_tables(obs_value, obs_error, obs_spot, obs_live, batch_colour, after):
    return pl.pallas_call(
        table_kernel,
        out_shape=(
            jax.ShapeDtypeStruct((ANALYSES, LANES, LANES), F32),
            jax.ShapeDtypeStruct((ANALYSES, 8, LANES), F32),
            jax.ShapeDtypeStruct((8, LANES), jnp.int32),
        ),
        in_specs=[SMEM] + [VMEM] * 4 + [HBM],
        out_specs=(VMEM, VMEM, VMEM),
        scratch_shapes=[pltpu.VMEM((LANES, LANES), F32)],
        compiler_params=params(),
        cost_estimate=weight(3),
        name="slot_tables",
    )(batch_colour, obs_value, obs_error, obs_spot, obs_live, after)


def shards(
    head_ensemble,
    transmissivity_grid,
    interlayer_leakage_factor,
    specific_porosity_release,
    infiltration_inflow,
    obs_value,
    obs_error,
    obs_spot,
    obs_live,
    batch_colour,
):
    heads = head_ensemble.reshape(LANES, ROWS, COLS)
    tiles, give_even, give_odd = edges(
        heads, transmissivity_grid, interlayer_leakage_factor, specific_porosity_release, infiltration_inflow
    )
    ns_odd, ns_even = swap(give_odd, "north", 1), swap(give_even, "north", 0)
    turned, give_even, give_odd = turn(heads.reshape(LANES * ROWS, COLS), tiles)
    ew_odd, ew_even = swap(give_odd, "east", 1), swap(give_even, "east", 0)
    give_even, give_odd = corners(ns_even, ns_odd)
    corner_odd, corner_even = swap(give_odd, "east", 1), swap(give_even, "east", 0)
    guides = slot_tables(obs_value, obs_error, obs_spot, obs_live, batch_colour, give_even)
    pieces = (turned, tiles, ns_even, ns_odd, ew_even, ew_odd, corner_even, corner_odd)
    cast, slots, ext_tiles = first_forecast(pieces, guides[2])
    gathered = gather_slots(slots)
    cast, slots = middle(guides, gathered, ext_tiles, cast)
    gathered = gather_slots(slots)
    out = last(guides, gathered, cast)
    return out.reshape(2, MEMBERS, ROWS, COLS)


def solution(mesh):
    placed = (
        P(None, None, "north", "east"),
        P(None, "north", "east"),
        P("north", "east"),
        P("north", "east"),
        P("north", "east"),
        P(),
        P(),
        P(),
        P(),
        P(),
    )
    return jax.shard_map(
        shards,
        mesh=mesh,
        in_specs=placed,
        out_specs=P(None, None, "north", "east"),
        check_vma=False,
    )
```

```python
import jax
import jax.numpy as jnp
from jax import lax
from jax.experimental import pallas as pl
from jax.experimental.pallas import tpu as pltpu
from jax.sharding import PartitionSpec as P

ITERS = 3
ANALYSES = 2
BATCHES = 4
MEMBERS = 64
RADIUS = 8
SPAN = 16
LOWER_WEIGHT = 0.6
LANES = 128

ROWS = 32
COLS = 128
HALO = 6
EDGE = 8
SKIRT = 3
EXT_ROWS = ROWS + 2 * HALO
EXT_COLS = COLS + 2 * EDGE
WIDE_COLS = EXT_COLS + 2 * EDGE
SIDE = 24
PAD_ROWS = 80
PAD_COLS = 184
CELL_ROWS = 6
CELL_COLS = 12
SLOTS = CELL_ROWS * CELL_COLS
OWN_ROWS = 2
OWN_COLS = 8
OWN = OWN_ROWS * OWN_COLS
GROUP_COLS = 48
KINDS = 8
WINDOW = 2 * RADIUS - 1

VMEM_BYTES = 64 * 2**20

F32 = jnp.float32
BF16 = jnp.bfloat16
SMEM = pl.BlockSpec(memory_space=pltpu.SMEM)
VMEM = pl.BlockSpec(memory_space=pltpu.VMEM)
HBM = pl.BlockSpec(memory_space=pltpu.HBM)
MARKS = pltpu.SMEM((8, LANES), jnp.int32)


def params():
    return pltpu.CompilerParams(vmem_limit_bytes=VMEM_BYTES)


def weight(microseconds):
    return pl.CostEstimate(flops=0, bytes_accessed=int(microseconds * 3.5e6), transcendentals=0)


def parity(axis):
    return lax.axis_index(axis) % 2


def edge_kernel(top, bottom, transmissivity, leakage, release, inflow, tiles, give_even, give_odd, stacked):
    stacked[...] = jnp.zeros_like(stacked)
    for half in range(2):
        part = slice(half * SPAN, (half + 1) * SPAN)
        for kind, field in enumerate((transmissivity.at[0], transmissivity.at[1], leakage, release, inflow)):
            stacked[pl.ds(half * LANES + kind, SPAN, stride=KINDS), :] = field[part, :]
        tiles[half] = stacked[half * LANES : (half + 1) * LANES, :].T
    odd = parity("north")
    for row in range(HALO):
        upper = top[pl.ds(row, LANES, stride=8), :].T
        lower = bottom[pl.ds(8 - HALO + row, LANES, stride=8), :].T
        give_even[row] = jnp.where(odd == 0, lower, upper)
        give_odd[row] = jnp.where(odd == 0, upper, lower)
    give_even[HALO] = tiles[1 - odd]
    give_odd[HALO] = tiles[odd]


def edges(heads, transmissivity, leakage, release, inflow):
    def rows_at(at):
        return pl.BlockSpec((LANES, 8, COLS), lambda i: (0, at, 0))

    def kernel(top, bottom, *rest):
        edge_kernel(top.reshape(LANES * 8, COLS), bottom.reshape(LANES * 8, COLS), *rest)

    halo = jax.ShapeDtypeStruct((HALO + 1, COLS, LANES), F32)
    return pl.pallas_call(
        kernel,
        grid=(1,),
        out_shape=(jax.ShapeDtypeStruct((2, COLS, LANES), F32), halo, halo),
        in_specs=[rows_at(0), rows_at(ROWS // 8 - 1)] + [VMEM] * 4,
        out_specs=(VMEM, VMEM, VMEM),
        scratch_shapes=[pltpu.VMEM((2 * LANES, COLS), F32)],
        compiler_params=params(),
        name="edges",
    )(heads, heads, transmissivity, leakage, release, inflow)


def turn_kernel(heads, tiles, turned, give_even, give_odd):
    def body(row, carry):
        turned[row] = heads[pl.ds(row, LANES, stride=ROWS), :].T
        return carry

    lax.fori_loop(0, ROWS, body, 0, unroll=16)
    odd = parity("east")
    for give, at in ((give_even, 1 - odd), (give_odd, odd)):
        cols = pl.ds(pl.multiple_of(at * (COLS - EDGE), EDGE), EDGE)
        give[:ROWS] = turned[:, cols, :]
        give[ROWS:] = tiles[:, cols, :]


def turn(heads, tiles):
    strip = jax.ShapeDtypeStruct((ROWS + 2, EDGE, LANES), F32)
    return pl.pallas_call(
        turn_kernel,
        out_shape=(jax.ShapeDtypeStruct((ROWS, COLS, LANES), F32), strip, strip),
        in_specs=[VMEM, VMEM],
        out_specs=(VMEM, VMEM, VMEM),
        compiler_params=params(),
        cost_estimate=weight(4),
        name="turn",
    )(heads, tiles)


def corner_kernel(even_left, even_right, odd_left, odd_right, after, give_even, give_odd):
    flip_n = parity("north") == 0
    flip_e = parity("east") == 0
    for half, swap_n in enumerate((flip_n, jnp.logical_not(flip_n))):
        left = jnp.where(swap_n, odd_left[...], even_left[...])
        right = jnp.where(swap_n, odd_right[...], even_right[...])
        part = slice(half * (HALO + 1), (half + 1) * (HALO + 1))
        give_even[part] = jnp.where(flip_e, right, left)
        give_odd[part] = jnp.where(flip_e, left, right)


def corners(got_even, got_odd, after):
    def cut(at):
        return pl.BlockSpec((HALO + 1, EDGE, LANES), lambda i: (0, at, 0))

    last = COLS // EDGE - 1
    whole = pl.BlockSpec((2 * HALO + 2, EDGE, LANES), lambda i: (0, 0, 0))
    shape = jax.ShapeDtypeStruct((2 * HALO + 2, EDGE, LANES), F32)
    return pl.pallas_call(
        corner_kernel,
        grid=(1,),
        out_shape=(shape, shape),
        in_specs=[cut(0), cut(last), cut(0), cut(last), HBM],
        out_specs=(whole, whole),
        compiler_params=params(),
        name="corners",
    )(got_even, got_even, got_odd, got_odd, after)


def spread_matrix():
    lane = lax.broadcasted_iota(jnp.int32, (2 * LANES, 4 * LANES), 0) % KINDS
    out = lax.broadcasted_iota(jnp.int32, (2 * LANES, 4 * LANES), 1)
    group = out // LANES
    lower = out % LANES >= MEMBERS
    wanted = jnp.where(group == 0, jnp.where(lower, 1, 0), group + 1)
    wanted = jnp.where((group == 3) & lower, KINDS, wanted)
    return (lane == wanted).astype(BF16)


def spread_rows(tiles, coef, matrix, first, rows):
    owner = lax.broadcasted_iota(jnp.int32, (EXT_COLS, LANES), 1) // KINDS
    parts = []
    for row in rows:
        parts.append(jnp.where(owner == (row + SPAN) % SPAN, tiles[(row + SPAN) // SPAN], 0.0))
    tile = jnp.concatenate(parts, axis=0)
    high = tile.astype(BF16)
    low = (tile - high.astype(F32)).astype(BF16)
    wide = jnp.dot(jnp.concatenate([high, low], axis=1), matrix, preferred_element_type=F32)
    for i, row in enumerate(rows):
        for kind in range(4):
            coef[kind, row - first] = wide[i * EXT_COLS : (i + 1) * EXT_COLS, kind * LANES : (kind + 1) * LANES]


def storage(u, around, start, factors):
    lateral, leakage, release, inflow = factors
    exchange = pltpu.roll(u, MEMBERS, 1) - u
    top = lateral * (around - 4.0 * u) + leakage * exchange + inflow
    bottom = release * (1.0 + jnp.tanh(0.5 * u)) + 1.0
    return start + top * pltpu.reciprocal(bottom, approx=True)


def storage_step(src, src_at, start, start_at, dst, dst_at, coef, coef_at, low, high, first, count, unroll=None):
    def strip(tile, carry):
        col = tile * 8 if unroll is None else pl.multiple_of(tile * 8, 8)

        def read(ref, at, row, shift=0):
            return ref[row + at[0], pl.ds(at[1] + 8 * first + shift + col, 8), :]

        above, u = read(src, src_at, low - 1), read(src, src_at, low)
        for row in range(low, high):
            below = read(src, src_at, row + 1)
            around = (above + below) + (read(src, src_at, row, -1) + read(src, src_at, row, 1))
            held = u if start is None else read(start, start_at, row)
            factors = [coef[kind, row + coef_at, pl.ds(EDGE + 8 * first + col, 8), :] for kind in range(4)]
            dst[row + dst_at[0], pl.ds(dst_at[1] + 8 * first + col, 8), :] = storage(u, around, held, factors)
            above, u = u, below
        return carry

    if unroll is None:
        for tile in range(count):
            strip(tile, 0)
    else:
        lax.fori_loop(0, count, strip, 0, unroll=unroll)


def fetch(pairs, sems):
    copies = [pltpu.make_async_copy(a, b, sems.at[i]) for i, (a, b) in enumerate(pairs)]
    for copy in copies:
        copy.start()
    return copies


def wait_for(copies):
    for copy in copies:
        copy.wait()


def first_kernel(
    turned, tiles, ns_even, ns_odd, ew_even, ew_odd, corner_even, corner_odd, marks_in,
    cast, slots, ext_tiles, start, one, two, coef, marks, tile_sems, sems,
):
    odd_n, odd_e = parity("north"), parity("east")
    even_row = (1 - odd_n) * (ROWS + HALO)
    odd_row = odd_n * (ROWS + HALO)
    even_col = (1 - odd_e) * (COLS + EDGE)
    odd_col = odd_e * (COLS + EDGE)
    inner = pl.ds(2 * EDGE, COLS)
    tile_inner = pl.ds(EDGE, COLS)
    moves = [
        (turned, start.at[pl.ds(HALO, ROWS), inner, :]),
        (ns_even.at[pl.ds(0, HALO)], start.at[pl.ds(even_row, HALO), inner, :]),
        (ns_odd.at[pl.ds(0, HALO)], start.at[pl.ds(odd_row, HALO), inner, :]),
    ]
    tile_moves = [
        (tiles, ext_tiles.at[pl.ds(1, 2), tile_inner, :]),
        (ns_even.at[pl.ds(HALO, 1)], ext_tiles.at[pl.ds((1 - odd_n) * 3, 1), tile_inner, :]),
        (ns_odd.at[pl.ds(HALO, 1)], ext_tiles.at[pl.ds(odd_n * 3, 1), tile_inner, :]),
    ]
    for at, strip, corner in ((even_col, ew_even, corner_even), (odd_col, ew_odd, corner_odd)):
        outer = pl.ds(pl.multiple_of(at + EDGE, EDGE), EDGE)
        tile_outer = pl.ds(pl.multiple_of(at, EDGE), EDGE)
        moves += [
            (strip.at[pl.ds(0, ROWS)], start.at[pl.ds(HALO, ROWS), outer, :]),
            (corner.at[pl.ds(0, HALO)], start.at[pl.ds(0, HALO), outer, :]),
            (corner.at[pl.ds(HALO + 1, HALO)], start.at[pl.ds(HALO + ROWS, HALO), outer, :]),
        ]
        tile_moves += [
            (strip.at[pl.ds(ROWS, 2)], ext_tiles.at[pl.ds(1, 2), tile_outer, :]),
            (corner.at[pl.ds(HALO, 1)], ext_tiles.at[pl.ds(0, 1), tile_outer, :]),
            (corner.at[pl.ds(2 * HALO + 1, 1)], ext_tiles.at[pl.ds(3, 1), tile_outer, :]),
        ]
    tile_copies = fetch(tile_moves, tile_sems)
    copies = fetch(moves + [(marks_in, marks)], sems)
    matrix = spread_matrix()
    wait_for(tile_copies)
    wait_for(copies)
    at = (HALO, 2 * EDGE)
    count = EXT_COLS // 8
    owner = lax.broadcasted_iota(jnp.int32, (GROUP_COLS, LANES), 1) // KINDS

    def body(group, carry):
        col = pl.multiple_of(group * GROUP_COLS, GROUP_COLS)
        needed = range(1 - HALO, ROWS + HALO - 1)
        parts = []
        for row in needed:
            tile = ext_tiles[(row + SPAN) // SPAN, pl.ds(col, GROUP_COLS), :]
            parts.append(jnp.where(owner == (row + SPAN) % SPAN, tile, 0.0))
        tile = jnp.concatenate(parts, axis=0)
        high = tile.astype(BF16)
        low = (tile - high.astype(F32)).astype(BF16)
        wide = jnp.dot(jnp.concatenate([high, low], axis=1), matrix, preferred_element_type=F32)
        for piece in range(GROUP_COLS // 8):
            aside = EDGE + 8 * piece
            above = start[0, pl.ds(col + aside, 8), :]
            u = start[1, pl.ds(col + aside, 8), :]
            for i, row in enumerate(needed):
                at_row = row + HALO
                below = start[at_row + 1, pl.ds(col + aside, 8), :]
                left = start[at_row, pl.ds(col + aside - 1, 8), :]
                right = start[at_row, pl.ds(col + aside + 1, 8), :]
                block = i * GROUP_COLS + 8 * piece
                factors = [wide[block : block + 8, kind * LANES : (kind + 1) * LANES] for kind in range(4)]
                for kind in range(4):
                    coef[kind, at_row, pl.ds(col + 8 * piece, 8), :] = factors[kind]
                one[at_row, pl.ds(col + aside, 8), :] = storage(u, (above + below) + (left + right), u, factors)
                above, u = u, below
        return carry

    lax.fori_loop(0, EXT_COLS // GROUP_COLS, body, 0)
    storage_step(one, at, start, at, two, at, coef, HALO, -4, ROWS + 4, -1, count, 9)
    copies = []
    for part in range(3):
        first = -1 + part * count // 3
        storage_step(two, at, start, at, one, at, coef, HALO, -SKIRT, ROWS + SKIRT, first, count // 3, 6)
        copy = pltpu.make_async_copy(
            one.at[pl.ds(HALO - SKIRT, ROWS + 2 * SKIRT), pl.ds(2 * EDGE + 8 * first, 8 * count // 3), :],
            cast.at[:, pl.ds(EDGE + 8 * first, 8 * count // 3), :],
            sems.at[part],
        )
        copy.start()
        copies.append(copy)
    pick_slots(one, at, marks, 0, slots)
    wait_for(copies)


def first_forecast(pieces, marks):
    return pl.pallas_call(
        first_kernel,
        out_shape=(
            jax.ShapeDtypeStruct((ROWS + 2 * SKIRT, EXT_COLS, LANES), F32),
            jax.ShapeDtypeStruct((OWN, LANES), F32),
            jax.ShapeDtypeStruct((4, EXT_COLS, LANES), F32),
        ),
        in_specs=[HBM] * 9,
        out_specs=(HBM, VMEM, VMEM),
        scratch_shapes=[pltpu.VMEM((EXT_ROWS, WIDE_COLS, LANES), F32)] * 3
        + [pltpu.VMEM((4, EXT_ROWS, EXT_COLS, LANES), F32)]
        + [MARKS, pltpu.SemaphoreType.DMA((9,)), pltpu.SemaphoreType.DMA((10,))],
        compiler_params=params(),
        name="first_forecast",
    )(*pieces, marks)


def pick_slots(src, at, marks, cycle, out):
    for slot in range(OWN):
        cell = (2 + slot // OWN_COLS) * CELL_COLS + 2 + slot % OWN_COLS
        out[slot : slot + 1, :] = src[marks[cycle, cell] + at[0], pl.ds(marks[2 + cycle, cell] + at[1], 1), :]


def halves(x):
    high = x.astype(BF16)
    return high, (x - high.astype(F32)).astype(BF16)


def serial_slots(cycle, mid, got_even, got_odd, tables, acrosses, members, anomaly, change, beside=None):
    table = tables[cycle, :SLOTS, :]
    across = acrosses[cycle]
    odd = parity("north") == 1
    south = jnp.where(odd, got_odd[...], got_even[...])
    north = jnp.where(odd, got_even[...], got_odd[...])
    flip = parity("east") == 0
    for third, source in enumerate((north, mid[...], south)):
        first, final = source[:OWN], source[2 * OWN :]
        west, east = jnp.where(flip, final, first), jnp.where(flip, first, final)
        for half in range(OWN_ROWS):
            base = (third * OWN_ROWS + half) * CELL_COLS
            own = half * OWN_COLS
            members[base : base + 2, :] = west[own + OWN_COLS - 2 : own + OWN_COLS]
            members[base + 2 : base + 2 + OWN_COLS, :] = source[OWN + own : OWN + own + OWN_COLS]
            members[base + 2 + OWN_COLS : base + CELL_COLS, :] = east[own : own + 2]
    lane = lax.broadcasted_iota(jnp.int32, (SLOTS, LANES), 1)
    prior = members[...]
    prior = jnp.where(lane < MEMBERS, prior, pltpu.roll(prior, MEMBERS, 1))
    value, noise, live = table[:, 0:1], table[:, 1:2], table[:, 2:3]
    near = jnp.maximum(0.0, 1.0 - jnp.abs(table[:, 3:4] - across[3:4, :]) / RADIUS)
    near = near * jnp.maximum(0.0, 1.0 - jnp.abs(table[:, 4:5] - across[4:5, :]) / RADIUS)
    turn_of = table[:, 5:6]
    spare = jnp.zeros((LANES - SLOTS, LANES), F32)
    kept_anomaly = jnp.zeros((SLOTS, LANES), F32)
    kept_change = jnp.zeros((SLOTS, LANES), F32)
    for batch in range(BATCHES):
        if beside is not None:
            beside(batch)
        now = turn_of == float(batch)
        mean = jnp.sum(prior, axis=1, keepdims=True) / LANES
        off = prior - mean
        spread = jnp.sum(off * off, axis=1, keepdims=True) / (2.0 * (MEMBERS - 1))
        gain = live / ((spread + noise) * (MEMBERS - 1))
        shrink = 1.0 / (1.0 + jnp.sqrt(noise / (spread + noise)))
        delta = jnp.where(now, gain * ((value - mean) - shrink * off), 0.0)
        kept_anomaly = jnp.where(now, off, kept_anomaly)
        kept_change = jnp.where(now, delta, kept_change)
        if batch < BATCHES - 1:
            high, low = halves(prior)
            off_high, off_low = halves(jnp.concatenate([off, spare], axis=0))
            cross = lax.dot_general(
                jnp.concatenate([high, high, low], axis=1),
                jnp.concatenate([off_high, off_low, off_high], axis=1),
                (((1,), (1,)), ((), ())),
                preferred_element_type=F32,
            )
            high, low = halves(0.5 * near * cross)
            delta_high, delta_low = halves(jnp.concatenate([delta, spare], axis=0))
            prior = prior + jnp.dot(
                jnp.concatenate([high, high, low], axis=1),
                jnp.concatenate([delta_high, delta_low, delta_high], axis=0),
                preferred_element_type=F32,
            )
    anomaly[...] = kept_anomaly
    change[...] = kept_change


def windows(cycle, marks, state, anomaly, change, skirt):
    lane_in = lax.broadcasted_iota(jnp.int32, (2 * LANES, LANES), 0) % LANES
    lane_out = lax.broadcasted_iota(jnp.int32, (2 * LANES, LANES), 1)
    ones = ((lane_in // MEMBERS) == (lane_out // MEMBERS)).astype(BF16)
    offset = lax.broadcasted_iota(jnp.int32, (2 * RADIUS, LANES), 0) - (RADIUS - 1)
    lane = lax.broadcasted_iota(jnp.int32, (2 * RADIUS, LANES), 1)
    taper = jnp.maximum(0.0, 1.0 - jnp.abs(offset).astype(F32) / RADIUS)
    taper = taper * jnp.where(lane < MEMBERS, 1.0, LOWER_WEIGHT)
    count = CELL_COLS // 2 - 1
    shift = SIDE - (RADIUS - 1)
    reach = RADIUS - 1 + skirt

    def batch_step(batch, carry):
        colour = marks[4 + cycle, batch]
        down, right = colour // 2, colour % 2
        own = (2 + down) * CELL_COLS + 2 - right
        other = (4 - 3 * down) * CELL_COLS + 2 - right
        edge = (1 - down) * (ROWS + skirt - reach) - down * skirt
        held, products, weights, places = [], [], [], []

        def visit(cell, row, col, pattern, height):
            x = state[row + SIDE, pl.ds(col, 2 * RADIUS), :]
            held.append(x)
            products.append(x * pattern)
            weights.append(height)
            places.append((cell, row + SIDE, col))

        for i in range(count):
            cell = own + 2 * i
            row, col = marks[cycle, cell] - (RADIUS - 1), marks[2 + cycle, cell] + shift
            pattern = anomaly[pl.ds(cell, 1), :]
            for step in range(WINDOW):
                visit(cell, row + step, col, pattern, 1.0 - abs(step - (RADIUS - 1)) / RADIUS)
        for i in range(count):
            cell = other + 2 * i
            row, col = marks[cycle, cell], marks[2 + cycle, cell] + shift
            pattern = anomaly[pl.ds(cell, 1), :]
            for step in range(reach):
                height = jnp.maximum(0.0, 1.0 - jnp.abs(edge + step - row).astype(F32) / RADIUS)
                visit(cell, edge + step, col, pattern, height)
        product = jnp.concatenate(products, axis=0)
        high = product.astype(BF16)
        low = (product - high.astype(F32)).astype(BF16)
        moment = jnp.dot(jnp.concatenate([high, low], axis=1), ones, preferred_element_type=F32)
        for n, (cell, row, col) in enumerate(places):
            part = moment[n * 2 * RADIUS : (n + 1) * 2 * RADIUS] * (taper * weights[n])
            state[row, pl.ds(col, 2 * RADIUS), :] = held[n] + part * change[pl.ds(cell, 1), :]
        return carry

    lax.fori_loop(0, BATCHES, batch_step, 0)


GUIDES = [
    pltpu.VMEM((ANALYSES, LANES, LANES), F32),
    pltpu.VMEM((ANALYSES, 8, LANES), F32),
    MARKS,
    pltpu.VMEM((3 * OWN, LANES), F32),
    pltpu.VMEM((3 * OWN, LANES), F32),
    pltpu.VMEM((3 * OWN, LANES), F32),
]


def middle_kernel(*refs):
    guides_in, (ext_in, cast, result, slots), refs = refs[:6], refs[6:10], refs[10:]
    guides, refs = refs[:6], refs[6:]
    tables, acrosses, marks, mid, got_even, got_odd = guides
    ext_tiles, state, members, anomaly, change, one, two, out, coef, sems, late = refs
    copies = fetch([*zip(guides_in, guides), (ext_in, ext_tiles)], sems)
    big_copy = pltpu.make_async_copy(
        cast, state.at[pl.ds(SIDE - SKIRT, ROWS + 2 * SKIRT), pl.ds(SIDE - EDGE, EXT_COLS), :], late.at[0]
    )
    big_copy.start()
    matrix = spread_matrix()
    wait_for(copies)

    def beside(batch):
        spread_rows(ext_tiles, coef, matrix, -2, range(-2 + batch * 9, 7 + batch * 9))

    serial_slots(0, mid, got_even, got_odd, tables, acrosses, members, anomaly, change, beside)
    big_copy.wait()
    windows(0, marks, state, anomaly, change, SKIRT)
    big = (SIDE, SIDE)
    at = (2, 2 * EDGE)
    storage_step(state, big, None, big, one, at, coef, 2, -2, ROWS + 2, -1, EXT_COLS // 8)
    storage_step(one, at, state, big, two, at, coef, 2, -1, ROWS + 1, -1, EXT_COLS // 8)
    copies = []
    for part in range(4):
        cols = pl.ds(part * COLS // 4, COLS // 4)
        storage_step(two, at, state, big, out, (0, 0), coef, 2, 0, ROWS, 4 * part, 4)
        copy = pltpu.make_async_copy(out.at[:, cols, :], result.at[:, cols, :], late.at[part])
        copy.start()
        copies.append(copy)
    pick_slots(out, (0, 0), marks, 1, slots)
    wait_for(copies)


def middle(guides, gathered, ext_tiles, cast):
    return pl.pallas_call(
        middle_kernel,
        out_shape=(
            jax.ShapeDtypeStruct((ROWS, COLS, LANES), F32),
            jax.ShapeDtypeStruct((OWN, LANES), F32),
        ),
        in_specs=[HBM] * 8,
        out_specs=(HBM, VMEM),
        scratch_shapes=GUIDES
        + [pltpu.VMEM((4, EXT_COLS, LANES), F32), pltpu.VMEM((PAD_ROWS, PAD_COLS, LANES), F32)]
        + [pltpu.VMEM((SLOTS, LANES), F32)] * 3
        + [pltpu.VMEM((ROWS + 4, WIDE_COLS, LANES), F32)] * 2
        + [pltpu.VMEM((ROWS, COLS, LANES), F32), pltpu.VMEM((4, ROWS + 4, EXT_COLS, LANES), F32)]
        + [pltpu.SemaphoreType.DMA((7,)), pltpu.SemaphoreType.DMA((4,))],
        compiler_params=params(),
        name="middle",
    )(*guides, *gathered, ext_tiles, cast)


def last_kernel(*refs):
    guides_in, (cast, heads), refs = refs[:6], refs[6:8], refs[8:]
    guides, refs = refs[:6], refs[6:]
    tables, acrosses, marks, mid, got_even, got_odd = guides
    state, members, anomaly, change, out, sems, late = refs
    copies = fetch([*zip(guides_in, guides)], sems)
    big_copy = pltpu.make_async_copy(cast, state.at[pl.ds(SIDE, ROWS), pl.ds(SIDE, COLS), :], late.at[0])
    big_copy.start()
    wait_for(copies)
    serial_slots(1, mid, got_even, got_odd, tables, acrosses, members, anomaly, change)
    big_copy.wait()
    windows(1, marks, state, anomaly, change, 0)
    copies = []
    for part in range(ROWS // 8):
        for i in range(8):
            block = state[part * 8 + i + SIDE, SIDE : SIDE + COLS, :].T
            out.at[part].reshape(LANES * 8, COLS)[pl.ds(i, LANES, stride=8), :] = block
        copy = pltpu.make_async_copy(out.at[part], heads.at[:, pl.ds(part * 8, 8), :], late.at[part])
        copy.start()
        copies.append(copy)
    wait_for(copies)


def last(guides, gathered, cast):
    return pl.pallas_call(
        last_kernel,
        out_shape=jax.ShapeDtypeStruct((LANES, ROWS, COLS), F32),
        in_specs=[HBM] * 7,
        out_specs=HBM,
        scratch_shapes=GUIDES
        + [pltpu.VMEM((PAD_ROWS, PAD_COLS, LANES), F32)]
        + [pltpu.VMEM((SLOTS, LANES), F32)] * 3
        + [pltpu.VMEM((ROWS // 8, LANES, 8, COLS), F32)]
        + [pltpu.SemaphoreType.DMA((6,)), pltpu.SemaphoreType.DMA((4,))],
        compiler_params=params(),
        name="last",
    )(*guides, *gathered, cast)


def swap(x, axis, odd):
    peers = lax.axis_size(axis)
    low = range(odd, peers - 1, 2)
    return lax.ppermute(x, axis, [(i, i + 1) for i in low] + [(i + 1, i) for i in low])


def gather_slots(slots):
    odd = swap(slots, "east", 1)
    even = swap(slots, "east", 0)
    mid = jnp.concatenate([even, slots, odd], axis=0)
    return mid, swap(mid, "north", 0), swap(mid, "north", 1)


def table_kernel(colours, value, noise, spot, live, after, tables, acrosses, marks, stacked):
    tall, wide = value.shape[2:]
    lat_row = lax.axis_index("north") - 1
    lat_col = lax.axis_index("east") * (COLS // (2 * SPAN)) - 1
    top = lax.Precision.HIGHEST
    spread = 2 * CELL_ROWS
    out_row = lax.broadcasted_iota(jnp.int32, (spread, tall), 0)
    in_row = lax.broadcasted_iota(jnp.int32, (spread, tall), 1)
    in_col = lax.broadcasted_iota(jnp.int32, (wide, LANES), 0)
    cell = lax.broadcasted_iota(jnp.int32, (wide, LANES), 1)
    take_col = (in_col == lat_col + cell % CELL_COLS // 2).astype(F32)
    got_row = lax.broadcasted_iota(jnp.int32, (spread, LANES), 0)
    lane = lax.broadcasted_iota(jnp.int32, (spread, LANES), 1)
    kept = (got_row // 2 == lane // CELL_COLS) & (got_row % 2 == lane % CELL_COLS % 2) & (lane < SLOTS)
    index = lax.broadcasted_iota(jnp.int32, (1, LANES), 1)
    cell_row, cell_col = index // CELL_COLS, index % CELL_COLS
    marks[...] = jnp.zeros_like(marks)
    for cycle in range(ANALYSES):
        turn = jnp.zeros((1, LANES), F32)
        rows_of = []
        for batch in range(BATCHES):
            colour = colours[cycle, batch]
            down, right = colour // 2, colour % 2
            wanted = (in_row == lat_row + out_row // 4) & (out_row // 2 % 2 == down) & (out_row % 2 == right)
            rows_of.append(wanted.astype(F32))
            mine = (cell_row % 2 == down) & (cell_col % 2 == right)
            turn = jnp.where(mine, float(batch), turn)
        picker = jnp.concatenate(rows_of, axis=1)
        fields = []
        for source in (value, noise, spot, live):
            whole = jnp.concatenate([source[cycle, batch].astype(F32) for batch in range(BATCHES)], axis=0)
            part = jnp.dot(picker, whole, precision=top, preferred_element_type=F32)
            part = jnp.dot(part, take_col, precision=top, preferred_element_type=F32)
            fields.append(jnp.sum(jnp.where(kept, part, 0.0), axis=0, keepdims=True))
        of_value, of_noise, of_spot, of_live = fields
        of_noise = jnp.where(of_noise > 0.0, of_noise, 1.0)
        place = (of_spot + 0.5).astype(jnp.int32)
        row = (cell_row - 2) * SPAN + place // SPAN
        col = (cell_col - 2) * SPAN + place % SPAN
        marks[cycle : cycle + 1, :] = row
        marks[2 + cycle : 3 + cycle, :] = col
        chosen = jnp.zeros((1, LANES), jnp.int32)
        for batch in range(BATCHES):
            chosen = jnp.where(index == batch, colours[cycle, batch], chosen)
        marks[4 + cycle : 5 + cycle, :] = chosen
        block = jnp.concatenate(
            [of_value, of_noise, of_live, row.astype(F32), col.astype(F32), turn, turn, turn], axis=0
        )
        acrosses[cycle] = block
        stacked[...] = jnp.zeros_like(stacked)
        stacked[:8, :] = block
        tables[cycle] = stacked[...].T


def slot_tables(obs_value, obs_error, obs_spot, obs_live, batch_colour, after):
    return pl.pallas_call(
        table_kernel,
        out_shape=(
            jax.ShapeDtypeStruct((ANALYSES, LANES, LANES), F32),
            jax.ShapeDtypeStruct((ANALYSES, 8, LANES), F32),
            jax.ShapeDtypeStruct((8, LANES), jnp.int32),
        ),
        in_specs=[SMEM] + [VMEM] * 4 + [HBM],
        out_specs=(VMEM, VMEM, VMEM),
        scratch_shapes=[pltpu.VMEM((LANES, LANES), F32)],
        compiler_params=params(),
        cost_estimate=weight(3),
        name="slot_tables",
    )(batch_colour, obs_value, obs_error, obs_spot, obs_live, after)


def shards(
    head_ensemble,
    transmissivity_grid,
    interlayer_leakage_factor,
    specific_porosity_release,
    infiltration_inflow,
    obs_value,
    obs_error,
    obs_spot,
    obs_live,
    batch_colour,
):
    heads = head_ensemble.reshape(LANES, ROWS, COLS)
    tiles, give_even, give_odd = edges(
        heads, transmissivity_grid, interlayer_leakage_factor, specific_porosity_release, infiltration_inflow
    )
    ns_odd, ns_even = swap(give_odd, "north", 1), swap(give_even, "north", 0)
    turned, give_even, give_odd = turn(heads.reshape(LANES * ROWS, COLS), tiles)
    ew_odd, ew_even = swap(give_odd, "east", 1), swap(give_even, "east", 0)
    guides = slot_tables(obs_value, obs_error, obs_spot, obs_live, batch_colour, give_even)
    give_even, give_odd = corners(ns_even, ns_odd, guides[2])
    corner_odd, corner_even = swap(give_odd, "east", 1), swap(give_even, "east", 0)
    pieces = (turned, tiles, ns_even, ns_odd, ew_even, ew_odd, corner_even, corner_odd)
    cast, slots, ext_tiles = first_forecast(pieces, guides[2])
    gathered = gather_slots(slots)
    cast, slots = middle(guides, gathered, ext_tiles, cast)
    gathered = gather_slots(slots)
    out = last(guides, gathered, cast)
    return out.reshape(2, MEMBERS, ROWS, COLS)


def solution(mesh):
    placed = (
        P(None, None, "north", "east"),
        P(None, "north", "east"),
        P("north", "east"),
        P("north", "east"),
        P("north", "east"),
        P(),
        P(),
        P(),
        P(),
        P(),
    )
    return jax.shard_map(
        shards,
        mesh=mesh,
        in_specs=placed,
        out_specs=P(None, None, "north", "east"),
        check_vma=False,
    )
```
